32 devices in a mesh: group: 8 (over y, x, core), tensor: 4 (over z).
Axes of the slice: x: 2, y: 2, z: 4, core: 2. Of those that a mesh axis runs over, the one named last changes fastest.
Arguments:
- left_table: bfloat16 [512, 8, 8192], P('group', 'tensor'), may hold values from -6 to 6
- right_table: bfloat16 [512, 8, 8192], P('group', 'tensor'), may hold values from -6 to 6
- left_owner: int32 [128, 1], P('group'), may hold values from 0 to 7; in each aligned block of 16 rows (0 to 15, 16 to 31, ...) at most 4 rows name the same one
- left_row: int32 [128], P('group'), may hold values from 0 to 63
- right_owner: int32 [128, 1], P('group'), may hold values from 0 to 7; in each aligned block of 16 rows (0 to 15, 16 to 31, ...) at most 4 rows name the same one
- right_row: int32 [128], P('group'), may hold values from 0 to 63
- pair_count: int32 [8], P('group'), may hold values from 1 to 16, 64 in all
- norm_gain: float32 [8192], replicated, may hold values from 0.1 to 1.9
- query_weight: bfloat16 [8192, 4096], P(None, 'tensor'), may hold values from -0.0625 to 0.0625
- key_weight: bfloat16 [8192, 1024], P(None, 'tensor'), may hold values from -0.0625 to 0.0625
- value_weight: bfloat16 [8192, 1024], P(None, 'tensor'), may hold values from -0.0625 to 0.0625
- output_weight: bfloat16 [4096, 8192], P('tensor'), may hold values from -0.09375 to 0.09375
Outputs:
- left_sums: float32 [512, 8192], P('group', 'tensor')
- right_sums: float32 [512, 8192], P('group', 'tensor')
The draws below stay inside these ranges and needn't reach their ends.
Inputs may be any that keep to these rules, and one draw needn't show every extreme that they name: `left_owner`: among the 16 pair slots of one group, at most 4 have the same left owner; some owner is named by exactly 4 of them in some groups. `right_owner`: among the 16 pair slots of one group, at most 4 have the same right owner; some owner is named by exactly 4 of them in some groups. `pair_count`: the counts sum to 64 and one group has all 16 slots live.
All inputs are finite; a program needn't handle non-finite values.
Results may differ from the reference program's by a relative error of at most 0.0035.
Values may be sent and summed in bfloat16 or wider, within the bound.
No kernel may reach another device: no remote copies, remote signals or barrier semaphores. Data moves between devices by JAX's collectives and lax.ppermute only.
A program may use at most 128 MiB of HBM per device.

```python
import math
import jax
import jax.numpy as jnp
import numpy as np
from jax import lax

D = 8192
HEADS = 32
KV_HEADS = 8
HEAD_DIM = 128
REC_TOKENS = 8
ROWS_DEV = 64
PAIRS_DEV = 16
PAIR_CAP = 4
TABLE_ROWS = 512
PAIRS = 128
N_GROUP = 8


def set_ends(entries, stream_key, least, largest):
    extent = entries.shape
    place = [jax.random.randint(jax.random.fold_in(stream_key, axis), (), 0, extent[axis]) for axis in range(len(extent))]
    entries = entries.at[tuple(place)].set(least)
    longest = extent.index(max(extent))
    place[longest] = (place[longest] + 1) % extent[longest]
    return entries.at[tuple(place)].set(largest)


def steps_of(own_key, dims, split, smallest, largest):
    factor_of = 1.0
    for axis_at, blocks in split:
        steps = jax.random.uniform(jax.random.fold_in(jax.random.fold_in(own_key, 6), axis_at), (blocks,), jnp.float32, smallest / len(split), largest / len(split))
        factor_of = factor_of * jnp.repeat(jnp.exp(steps), dims[axis_at] // blocks).reshape((-1,) + (1,) * (len(dims) - 1 - axis_at))
    return factor_of


def length_profile(count, total, most, skew):
    loads = [(1 << 20) // math.isqrt(rank ** skew) + 1 for rank in range(2, count + 1)]
    surplus, given = total - most - (count - 1), [1] * (count - 1)
    while surplus > 0:
        candidates = [i for i in range(count - 1) if given[i] < most]
        pool, budget = sum([loads[i] for i in candidates]), surplus
        for i in candidates:
            more = min(most - given[i], max(1, budget * loads[i] // pool), surplus)
            given[i] = given[i] + more
            surplus = surplus - more
    return np.array([most] + given)


def ragged(own_key, number_of, total, bound, slope):
    if number_of == 2:
        one = jax.random.randint(own_key, (), max(1, total - bound), min(bound, total - 1) + 1)
        return jnp.stack([one, total - one])
    lengths = jnp.asarray(length_profile(number_of, total, bound, slope), jnp.int32)
    pairs = (number_of - 1) // 2
    donor, receiver = lengths[1:1 + 2 * pairs:2], lengths[2:2 + 2 * pairs:2]
    margin = jnp.minimum(donor - 1, bound - receiver)
    moved = jax.random.randint(jax.random.fold_in(own_key, 1), (pairs,), 0, 1 << 20) % (margin + 1)
    lengths = lengths.at[1:1 + 2 * pairs:2].set(donor - moved).at[2:2 + 2 * pairs:2].set(receiver + moved)
    return lengths[jax.random.permutation(jax.random.fold_in(own_key, 2), number_of)]


def deal_out(rng, own, number, rows, amount, top, reach, slope):
    order = jax.random.permutation(rng, amount)
    crowded, common = load_shares(amount, rows * top, reach, slope, True), load_shares(amount, rows * top, reach, slope, False)
    places = jnp.arange(amount)

    def named(sizes, rotation):
        used = int((sizes > 0).sum())
        fixed = max(1, used // 4)
        passed = fixed + (places - fixed + rotation * (used - fixed)) % max(1, amount - fixed)
        return jnp.zeros((amount,), jnp.int32).at[order[jnp.where(places < fixed, places, passed)]].set(jnp.asarray(sizes, jnp.int32))

    sizes = jnp.where(number % 4 == 0, named(crowded, number // 4), named(common, number - number // 4 - 1))
    mixed = jax.random.permutation(jax.random.fold_in(own, 3), amount)
    donor, taker = mixed[0:amount // 2 * 2:2], mixed[1:amount // 2 * 2:2]
    slack = jnp.minimum(sizes[donor] - 1, reach - sizes[taker]) // 2
    slack = jnp.where((donor == order[0]) | (taker == order[0]) | (sizes[taker] == 0), 0, jnp.maximum(slack, 0))
    passed = jax.random.randint(jax.random.fold_in(own, 4), (amount // 2,), 0, 1 << 20) % (slack + 1)
    sizes = sizes.at[donor].add(-passed).at[taker].add(passed)
    labels = jnp.searchsorted(jnp.cumsum(sizes), jnp.arange(rows * top), side="right").astype(jnp.int32)
    table = labels.reshape(top, rows).T
    table = table[jax.random.permutation(jax.random.fold_in(own, 1), rows)]
    rotation = jax.random.randint(jax.random.fold_in(own, 2), (rows, 1), 0, top)
    return jnp.take_along_axis(table, (jnp.arange(top)[None, :] + rotation) % top, axis=1)


def load_shares(number_of, total, bound, skew, full):
    weights = [(1 << 20) // math.isqrt(grade ** skew) + 1 for grade in range(1, number_of + 1)]
    largest = bound if full else min(bound, max(-(-total // number_of), total * weights[0] // sum(weights)))
    least = 1 if total - largest >= number_of - 1 else 0
    given, rest = [largest] + [least] * (number_of - 1), total - largest - least * (number_of - 1)
    while rest > 0:
        movable = [i for i in range(1, number_of) if given[i] < largest] or [i for i in range(1, number_of) if given[i] < bound]
        pool, remaining = sum([weights[i] for i in movable]), rest
        for i in movable:
            more = min(bound - given[i], max(1, remaining * weights[i] // pool), rest)
            given[i] = given[i] + more
            rest = rest - more
    return np.array(given)


def centred(stream_key, extent, scale, bound, split=(), kind=jnp.bfloat16):
    array = jax.random.normal(stream_key, extent, jnp.float32) * scale
    if len(split) > 0:
        array = steps_of(stream_key, extent, split, -0.22, 0.18) * array
    return jnp.clip(array, min=-bound, max=bound).astype(kind)


def setup_inputs(seed: int = 0) -> dict:
    key_of = jax.random.split(jax.random.key(seed), 13)
    left_table = centred(key_of[0], (TABLE_ROWS, REC_TOKENS, D), 1.0, 6.0, ((0, 8), (1, 4)))
    right_table = centred(key_of[1], (TABLE_ROWS, REC_TOKENS, D), 1.0, 6.0, ((0, 8), (1, 4)))
    left_owner_keys = jax.random.split(jax.random.fold_in(key_of[2], 1), PAIRS // PAIRS_DEV)
    left_owner_turns = jax.random.permutation(jax.random.fold_in(key_of[2], 3), PAIRS // PAIRS_DEV)
    left_owner = jax.vmap(lambda own, number: deal_out(jax.random.fold_in(key_of[2], 2), own, number, PAIRS_DEV, N_GROUP, 1, PAIR_CAP, 2))(left_owner_keys, left_owner_turns).reshape((PAIRS, 1))
    left_row = set_ends(jax.random.randint(key_of[3], (PAIRS,), 0, ROWS_DEV), jax.random.fold_in(key_of[3], 1), 0, ROWS_DEV - 1).astype(jnp.int32)
    right_owner_keys = jax.random.split(jax.random.fold_in(key_of[4], 1), PAIRS // PAIRS_DEV)
    right_owner_turns = jax.random.permutation(jax.random.fold_in(key_of[4], 3), PAIRS // PAIRS_DEV)
    right_owner = jax.vmap(lambda own, number: deal_out(jax.random.fold_in(key_of[4], 2), own, number, PAIRS_DEV, N_GROUP, 1, PAIR_CAP, 2))(right_owner_keys, right_owner_turns).reshape((PAIRS, 1))
    right_row = set_ends(jax.random.randint(key_of[5], (PAIRS,), 0, ROWS_DEV), jax.random.fold_in(key_of[5], 1), 0, ROWS_DEV - 1).astype(jnp.int32)
    pair_count = ragged(key_of[6], N_GROUP, N_GROUP * PAIRS_DEV // 2, PAIRS_DEV, 2).astype(jnp.int32)
    norm_gain = jnp.clip(1.0 + 0.18 * jax.random.normal(key_of[7], (D,), jnp.float32), 0.1, 1.9)
    query_weight = centred(key_of[8], (D, HEADS * HEAD_DIM), D ** -0.5, 0.0625, ((1, 4),))
    key_weight = centred(key_of[9], (D, KV_HEADS * HEAD_DIM), D ** -0.5, 0.0625, ((1, 4),))
    value_weight = centred(key_of[10], (D, KV_HEADS * HEAD_DIM), D ** -0.5, 0.0625, ((1, 4),))
    output_weight = centred(key_of[11], (HEADS * HEAD_DIM, D), (HEADS * HEAD_DIM) ** -0.5, 0.09375, ((0, 4),))
    return dict(left_table=left_table, right_table=right_table, left_owner=left_owner, left_row=left_row, right_owner=right_owner, right_row=right_row, pair_count=pair_count, norm_gain=norm_gain, query_weight=query_weight, key_weight=key_weight, value_weight=value_weight, output_weight=output_weight)


score_scale = 4.0

def pair_states(left_tokens, right_tokens, norm_gain, query_weight, key_weight, value_weight, output_weight):
    inputs = jnp.concatenate([left_tokens, right_tokens], axis=1)
    count = inputs.shape[0]
    length = inputs.shape[1]
    flat = inputs.reshape(count * length, D).astype(jnp.float32)
    scale = lax.rsqrt(lax.optimization_barrier(jnp.mean(flat * flat, axis=-1, keepdims=True)) + 1e-05)
    normed = (flat * scale * norm_gain[None, :]).astype(jnp.bfloat16)
    q_raw = jnp.dot(normed, query_weight, preferred_element_type=jnp.float32)
    k_raw = jnp.dot(normed, key_weight, preferred_element_type=jnp.float32)
    values = jnp.dot(normed, value_weight, preferred_element_type=jnp.float32).astype(jnp.bfloat16)
    q_heads = q_raw.reshape(count * length, HEADS, HEAD_DIM)
    k_heads = k_raw.reshape(count * length, KV_HEADS, HEAD_DIM)
    q_norm = (q_heads * lax.rsqrt(lax.optimization_barrier(jnp.mean(q_heads * q_heads, axis=-1, keepdims=True)) + 1e-06)).astype(jnp.bfloat16)
    k_norm = (k_heads * lax.rsqrt(lax.optimization_barrier(jnp.mean(k_heads * k_heads, axis=-1, keepdims=True)) + 1e-06)).astype(jnp.bfloat16)
    share = HEADS // KV_HEADS
    q_five = q_norm.reshape(count, length, KV_HEADS, share, HEAD_DIM).astype(jnp.float32)
    k_four = k_norm.reshape(count, length, KV_HEADS, HEAD_DIM).astype(jnp.float32)
    v_four = values.reshape(count, length, KV_HEADS, HEAD_DIM).astype(jnp.float32)
    scores = jnp.einsum('pqkgd,pskd->pkgqs', q_five, k_four) * (score_scale / HEAD_DIM)
    expo = jnp.exp(scores)
    weights = (expo / lax.optimization_barrier(jnp.sum(expo, axis=-1, keepdims=True))).astype(jnp.bfloat16)
    context = jnp.einsum('pkgqs,pskd->pqkgd', weights.astype(jnp.float32), v_four).astype(jnp.bfloat16)
    context = context.reshape(count * length, HEADS * HEAD_DIM)
    attended = jnp.dot(context, output_weight, preferred_element_type=jnp.float32)
    total = flat + attended
    return lax.optimization_barrier(jnp.mean(total.reshape(count, length, D), axis=1))

def reference(left_table, right_table, left_owner, left_row, right_owner, right_row, pair_count, norm_gain, query_weight, key_weight, value_weight, output_weight):
    left_ids = (left_owner[:, 0] * ROWS_DEV + left_row).astype(jnp.int32)
    right_ids = (right_owner[:, 0] * ROWS_DEV + right_row).astype(jnp.int32)

    def one_group(ids):
        return pair_states(left_table[ids[0]], right_table[ids[1]], norm_gain, query_weight, key_weight, value_weight, output_weight)
    pooled = lax.map(one_group, (left_ids.reshape(N_GROUP, PAIRS_DEV), right_ids.reshape(N_GROUP, PAIRS_DEV)))
    pooled = pooled.reshape(N_GROUP * PAIRS_DEV, D)
    live = (jnp.arange(PAIRS_DEV, dtype=jnp.int32)[None, :] < pair_count[:, None]).reshape(N_GROUP * PAIRS_DEV)
    pooled = jnp.where(live[:, None], pooled, jnp.zeros_like(pooled))
    left_sums = jax.ops.segment_sum(pooled, left_ids, num_segments=ROWS_DEV * N_GROUP)
    right_sums = jax.ops.segment_sum(pooled, right_ids, num_segments=ROWS_DEV * N_GROUP)
    return (left_sums, right_sums)
```

```python
import functools

import jax
import jax.numpy as jnp
from jax import lax
from jax.experimental import pallas as pl
from jax.experimental.pallas import tpu as pltpu
from jax.sharding import PartitionSpec as P

HEAD_DIM = 128


score_scale = 4.0


def slot_plan(owner, groups, capacity):
    count = owner.shape[0]
    order = jnp.arange(count, dtype=jnp.int32)
    same_owner = owner[:, None] == owner[None, :]
    earlier = order[None, :] < order[:, None]
    rank = jnp.sum(jnp.logical_and(same_owner, earlier), axis=1)
    owner_hit = owner[:, None, None] == jnp.arange(groups, dtype=jnp.int32)[None, :, None]
    rank_hit = rank[:, None, None] == jnp.arange(capacity, dtype=jnp.int32)[None, None, :]
    return (rank, jnp.logical_and(owner_hit, rank_hit))


def request_ids(slot_match, row_index):
    return jnp.sum(jnp.where(slot_match, row_index[:, None, None], 0), axis=0)


def owner_sums(row_ids, arrived, rows_here):
    onehot = (row_ids[:, :, None] == jnp.arange(rows_here, dtype=jnp.int32)[None, None, :]).astype(
        jnp.float32
    )
    return jnp.einsum("gcr,gcf->rf", onehot, arrived, precision=lax.Precision.HIGHEST)


def general_program(
    left_table,
    right_table,
    left_owner,
    left_row,
    right_owner,
    right_row,
    pair_count,
    norm_gain,
    query_weight,
    key_weight,
    value_weight,
    output_weight,
):
    groups = lax.axis_size("group")
    tensors = lax.axis_size("tensor")
    pairs_here = left_owner.shape[0]
    capacity = 2 * pairs_here // groups
    rows_here = left_table.shape[0]
    width = left_table.shape[2]
    feature_share = width // tensors
    left_group = left_owner[:, 0]
    right_group = right_owner[:, 0]
    left_rank, left_match = slot_plan(left_group, groups, capacity)
    right_rank, right_match = slot_plan(right_group, groups, capacity)
    left_request = request_ids(left_match, left_row)
    right_request = request_ids(right_match, right_row)
    left_spread = jnp.broadcast_to(left_request[:, None, :], (groups, tensors, capacity)).reshape(
        groups * tensors, capacity
    )
    right_spread = jnp.broadcast_to(right_request[:, None, :], (groups, tensors, capacity)).reshape(
        groups * tensors, capacity
    )
    left_wanted, right_wanted = (
        lax.all_to_all(left_spread, ("group", "tensor"), split_axis=0, concat_axis=0, tiled=True),
        lax.all_to_all(right_spread, ("group", "tensor"), split_axis=0, concat_axis=0, tiled=True),
    )
    left_back, right_back = (
        lax.all_to_all(
            left_table[left_wanted], ("group", "tensor"), split_axis=0, concat_axis=0, tiled=True
        ),
        lax.all_to_all(
            right_table[right_wanted], ("group", "tensor"), split_axis=0, concat_axis=0, tiled=True
        ),
    )
    left_back = left_back.reshape(groups, tensors, capacity, left_table.shape[1], width)
    right_back = right_back.reshape(groups, tensors, capacity, right_table.shape[1], width)
    left_tokens = left_back[left_group, :, left_rank].reshape(
        pairs_here, tensors * left_table.shape[1], width
    )
    right_tokens = right_back[right_group, :, right_rank].reshape(
        pairs_here, tensors * right_table.shape[1], width
    )
    left_owned = left_wanted.reshape(groups, tensors, capacity)[:, 0]
    right_owned = right_wanted.reshape(groups, tensors, capacity)[:, 0]
    inputs = jnp.concatenate([left_tokens, right_tokens], axis=1)
    length = inputs.shape[1]
    flat = inputs.reshape(pairs_here * length, width)
    wide = flat.astype(jnp.float32)
    scale = lax.rsqrt(jnp.mean(wide * wide, axis=-1, keepdims=True) + 1e-05)
    normed = (wide * scale * norm_gain[None, :]).astype(jnp.bfloat16)
    q_raw = jnp.dot(normed, query_weight, preferred_element_type=jnp.float32)
    k_raw = jnp.dot(normed, key_weight, preferred_element_type=jnp.float32)
    values = jnp.dot(normed, value_weight, preferred_element_type=jnp.float32).astype(jnp.bfloat16)
    kv_local = key_weight.shape[1] // HEAD_DIM
    share = query_weight.shape[1] // HEAD_DIM // kv_local
    q_heads = q_raw.reshape(pairs_here * length, kv_local * share, HEAD_DIM)
    k_heads = k_raw.reshape(pairs_here * length, kv_local, HEAD_DIM)
    q_norm = (
        q_heads * lax.rsqrt(jnp.mean(q_heads * q_heads, axis=-1, keepdims=True) + 1e-06)
    ).astype(jnp.bfloat16)
    k_norm = (
        k_heads * lax.rsqrt(jnp.mean(k_heads * k_heads, axis=-1, keepdims=True) + 1e-06)
    ).astype(jnp.bfloat16)
    q_five = q_norm.reshape(pairs_here, length, kv_local, share, HEAD_DIM)
    k_four = k_norm.reshape(pairs_here, length, kv_local, HEAD_DIM)
    v_four = values.reshape(pairs_here, length, kv_local, HEAD_DIM)
    scores = jnp.einsum("pqkgd,pskd->pkgqs", q_five, k_four, preferred_element_type=jnp.float32) * (
        score_scale / HEAD_DIM
    )
    expo = jnp.exp(scores)
    weights = (expo / jnp.sum(expo, axis=-1, keepdims=True)).astype(jnp.bfloat16)
    context = jnp.einsum(
        "pkgqs,pskd->pqkgd", weights, v_four, preferred_element_type=jnp.float32
    ).astype(jnp.bfloat16)
    context = context.reshape(pairs_here * length, kv_local * share * HEAD_DIM)
    attended = jnp.dot(context, output_weight, preferred_element_type=jnp.float32)
    head_term = jnp.mean(attended.reshape(pairs_here, length, width), axis=1)
    head_part = lax.psum_scatter(head_term, "tensor", scatter_dimension=1, tiled=True)
    feature_start = lax.axis_index("tensor") * feature_share
    own_features = lax.dynamic_slice_in_dim(inputs, feature_start, feature_share, 2)
    residual_mean = jnp.mean(own_features.astype(jnp.float32), axis=1)
    live = jnp.arange(pairs_here, dtype=jnp.int32) < pair_count[0]
    pooled = jnp.where(live[:, None], residual_mean + head_part, jnp.zeros_like(head_part))
    left_send = jnp.einsum(
        "pgc,pf->gcf", left_match.astype(jnp.float32), pooled, precision=lax.Precision.HIGHEST
    )
    right_send = jnp.einsum(
        "pgc,pf->gcf", right_match.astype(jnp.float32), pooled, precision=lax.Precision.HIGHEST
    )
    left_got, right_got = (
        lax.all_to_all(left_send, "group", split_axis=0, concat_axis=0, tiled=True),
        lax.all_to_all(right_send, "group", split_axis=0, concat_axis=0, tiled=True),
    )
    left_sums = owner_sums(left_owned, left_got, rows_here)
    right_sums = owner_sums(right_owned, right_got, rows_here)
    return (left_sums, right_sums)

LANES = 128
DEAD = -1
RIGHT_SHIFT = 12
DEALS = 8
BF16 = jnp.bfloat16
F32 = jnp.float32


def log2(number):
    bits = number.bit_length() - 1
    assert 1 << bits == number
    return bits


def plan_sizes(groups, pairs_here):
    share = pairs_here // 2
    mean = -(-2 * share // groups)
    return (share, min(LANES // groups, 3 * mean))


def column(row):
    n = row.shape[1]
    return jnp.transpose(jnp.broadcast_to(row, (n, n)))[:, :1]


def split3(wide):
    high = wide.astype(BF16)
    rest = wide - high.astype(F32)
    mid = rest.astype(BF16)
    low = (rest - mid.astype(F32)).astype(BF16)
    return (high, mid, low)


def plan_body(codes, me, groups, share, cap, rows_here):
    n = codes.shape[1]
    gbits, rbits = log2(groups), log2(rows_here)
    live_total = groups * share
    live = codes >= 0
    left = jnp.where(live, codes & ((1 << RIGHT_SHIFT) - 1), 0)
    right = jnp.where(live, codes >> RIGHT_SHIFT, 0)
    left_own, right_own = left >> rbits, right >> rbits
    order = lax.broadcasted_iota(jnp.int32, (1, n), 1)
    owners = lax.broadcasted_iota(jnp.int32, (groups, n), 0)
    load_of = (left_own == owners).astype(F32) + (right_own == owners).astype(F32)
    load_of = jnp.where(live, load_of, 0.0).astype(BF16)
    live_c, left_c, right_c = column(live.astype(jnp.int32)), column(left), column(right)
    lo_c, ro_c = left_c >> rbits, right_c >> rbits
    order_c = lax.broadcasted_iota(jnp.int32, (n, 1), 0)

    def key(low, rown, alive, at, turn):
        second = (rown + turn * low) & (groups - 1)
        return jnp.where(alive, ((low << gbits) + second) * n, groups * groups * n) + at

    best, best_load = None, None
    for turn in range(DEALS):
        key_r = key(left_own, right_own, live, order, turn)
        key_c = key(lo_c, ro_c, live_c > 0, order_c, turn)
        rank = jnp.sum((key_c < key_r).astype(jnp.int32), axis=0, keepdims=True)
        to = jnp.where(rank < live_total, rank & (groups - 1), groups)
        hit = (to == owners).astype(BF16)
        load = lax.dot_general(hit, load_of, (((1,), (1,)), ((), ())), preferred_element_type=F32)
        most = jnp.max(jnp.max(load, axis=1, keepdims=True), axis=0, keepdims=True)
        if best is None:
            best, best_load = rank, most
        else:
            better = most < best_load
            best = jnp.where(better, rank, best)
            best_load = jnp.where(better, most, best_load)
    rank = best
    rank_c = column(rank)
    to_c = jnp.where(rank_c < live_total, rank_c & (groups - 1), groups)
    slot_c = rank_c >> gbits
    to = jnp.where(rank < live_total, rank & (groups - 1), groups)
    same_to = to_c == to
    earlier = jnp.logical_and(same_to, rank < rank_c)

    def count(mask):
        return jnp.sum(mask.astype(jnp.int32), axis=1, keepdims=True)

    left_pos = count(jnp.logical_and(earlier, lo_c == left_own))
    right_pos = count(jnp.logical_and(earlier, ro_c == right_own)) + count(
        jnp.logical_and(jnp.logical_and(same_to, rank < live_total), ro_c == left_own)
    )
    lane = lax.broadcasted_iota(jnp.int32, (n, LANES), 1)
    alive = rank_c < live_total

    def place(mask, at, value):
        return jnp.sum(
            jnp.where(jnp.logical_and(mask, at == lane), value, 0), axis=0, keepdims=True
        )

    left_in = jnp.logical_and(alive, left_pos < cap)
    right_in = jnp.logical_and(alive, right_pos < cap)
    local_left, local_right = left_c & (rows_here - 1), right_c & (rows_here - 1)
    send = place(
        jnp.logical_and(left_in, lo_c == me), to_c * cap + left_pos, local_left
    ) + place(
        jnp.logical_and(right_in, ro_c == me), to_c * cap + right_pos, local_right + rows_here
    )
    mine = jnp.logical_and(alive, to_c == me)
    fetch = place(
        jnp.logical_and(mine, left_in), slot_c * 2, lo_c * cap + left_pos
    ) + place(jnp.logical_and(mine, right_in), slot_c * 2 + 1, ro_c * cap + right_pos)
    back = to_c * share + slot_c
    left_row = place(jnp.logical_and(alive, lo_c == me), back, local_left + 1) - 1
    right_row = place(jnp.logical_and(alive, ro_c == me), back, local_right + 1) - 1
    over = jnp.broadcast_to((best_load > cap).astype(jnp.int32), (1, LANES))
    return (send, fetch, left_row, right_row, over)


def copy_rows(index_of, source_of, target, sems, number, start):
    for cell in range(number):
        index = index_of(cell)
        start(index, cell, target.at[cell], sems.at[cell])


def gather_cells(plan, left, right, out, sems, rows_here, cells, first, wide):
    def one(cell, begin):
        index = plan[0, cell]
        row = index & (rows_here - 1)
        for side, table in ((0, left), (1, right)):

            @pl.when((index >= rows_here) == (side == 1))
            def _():
                copy = pltpu.make_async_copy(
                    table.at[row, :, pl.ds(first, wide)], out.at[cell], sems.at[cell]
                )
                copy.start()

    lax.fori_loop(0, cells, lambda cell, carry: (one(cell, True), carry)[1], 0)

    def finish(cell, carry):
        pltpu.make_async_copy(
            left.at[0, :, pl.ds(first, wide)], out.at[cell], sems.at[cell]
        ).wait()
        return carry

    lax.fori_loop(0, cells, finish, 0)


def plan_kernel(groups, share, cap, rows_here, wide, me, codes, left, right, plan_out, out, plan, sem, sems):
    rows = jnp.sum(codes[...], axis=0, keepdims=True)
    table = plan_body(rows, me[0], groups, share, cap, rows_here)
    for at, row in enumerate(table):
        plan_out[pl.ds(at, 1), :] = row
    copy = pltpu.make_async_copy(plan_out, plan, sem)
    copy.start()
    copy.wait()
    gather_cells(plan, left, right, out, sems, rows_here, groups * cap, 0, wide)


def gather_kernel(rows_here, cells, first, wide, plan, left, right, out, sems):
    gather_cells(plan, left, right, out, sems, rows_here, cells, first, wide)


def pick_kernel(items, plan, got, out, held, sems):
    def begin(item, carry):
        pltpu.make_async_copy(got.at[plan[1, item]], held.at[item], sems.at[item]).start()
        return carry

    def finish(item, carry):
        pltpu.make_async_copy(got.at[0], held.at[item], sems.at[item]).wait()
        return carry

    lax.fori_loop(0, items, begin, 0)
    lax.fori_loop(0, items, finish, 0)
    out[...] = held[...].reshape(out.shape)


def qkv_kernel(first, resid, pair_rows, *refs):
    refs = list(refs)
    x_ref, gain, wq, wk, wv = refs[:5]
    refs = refs[5:]
    if not first:
        acc_in, sq_in = refs[:2]
        refs = refs[2:]
    acc, sq = refs[:2]
    step = pl.program_id(0)
    x = x_ref[...]
    wide = x.astype(F32)
    normed = (wide * gain[...]).astype(BF16)
    q = jnp.dot(normed, wq[...], preferred_element_type=F32)
    k = jnp.dot(normed, wk[...], preferred_element_type=F32)
    v = jnp.dot(normed, wv[...], preferred_element_type=F32)
    square = jnp.broadcast_to(jnp.sum(wide * wide, axis=1, keepdims=True), sq.shape)
    nq, nk = q.shape[1], k.shape[1]

    @pl.when(step == 0)
    def _():
        if first:
            acc[...] = jnp.zeros_like(acc)
            sq[...] = jnp.zeros_like(sq)
        else:
            acc[...] = acc_in[...]
            sq[...] = sq_in[...]

    acc[:, :nq] += q
    acc[:, nq : nq + nk] += k
    acc[:, nq + nk :] += v
    sq[...] += square
    if resid:
        rows = x.shape[0]
        pairs = rows // pair_rows
        pair = lax.broadcasted_iota(jnp.int32, (pairs, rows), 1) // pair_rows
        mine = (pair == lax.broadcasted_iota(jnp.int32, (pairs, rows), 0)).astype(BF16)
        refs[2][...] = jnp.dot(mine, x, preferred_element_type=F32)


def attend_kernel(width, length, pair_rows, heads, kv_heads, *refs):
    shards = (len(refs) - 5) // 2
    t_ref = refs[0]
    accs, sqs = refs[1 : 1 + shards], refs[1 + shards : 1 + 2 * shards]
    resid, wo, out, ctx = refs[1 + 2 * shards :]
    pairs = out.shape[1]

    @pl.when(pl.program_id(0) == 0)
    def _():
        acc = jnp.concatenate([a[...] for a in accs], axis=0)
        sq = jnp.concatenate([s[...] for s in sqs], axis=0)[:, :1]
        tokens = acc.shape[0]
        scale = lax.rsqrt(sq * (1.0 / width) + 1e-05)
        acc = acc * scale
        rows = tokens // shards
        row = lax.broadcasted_iota(jnp.int32, (tokens, tokens), 0)
        col = lax.broadcasted_iota(jnp.int32, (tokens, tokens), 1)
        same = ((row & (rows - 1)) >> log2(pair_rows)) == ((col & (rows - 1)) >> log2(pair_rows))
        pair = lax.broadcasted_iota(jnp.int32, (pairs, tokens), 0)
        token = lax.broadcasted_iota(jnp.int32, (pairs, tokens), 1)
        member = ((token & (rows - 1)) >> log2(pair_rows)) == pair
        nq = heads * HEAD_DIM
        nk = kv_heads * HEAD_DIM

        def unit(part):
            return (
                part * lax.rsqrt(jnp.mean(part * part, axis=1, keepdims=True) + 1e-06)
            ).astype(BF16)

        for kv in range(kv_heads):
            k = unit(acc[:, nq + kv * HEAD_DIM : nq + (kv + 1) * HEAD_DIM])
            v = acc[:, nq + nk + kv * HEAD_DIM : nq + nk + (kv + 1) * HEAD_DIM].astype(BF16)
            for part in range(heads // kv_heads):
                head = kv * (heads // kv_heads) + part
                q = unit(acc[:, head * HEAD_DIM : (head + 1) * HEAD_DIM])
                scores = lax.dot_general(
                    q, k, (((1,), (1,)), ((), ())), preferred_element_type=F32
                ) * (score_scale / HEAD_DIM)
                expo = jnp.where(same, jnp.exp(scores), 0.0)
                weights = expo / jnp.sum(expo, axis=1, keepdims=True)
                mean = jnp.sum(weights, axis=0, keepdims=True) * (1.0 / length)
                spread = jnp.where(member, mean, 0.0)
                high = spread.astype(BF16)
                low = (spread - high.astype(F32)).astype(BF16)
                context = jnp.dot(
                    jnp.concatenate([high, low], axis=0), v, preferred_element_type=F32
                )
                context = context[:pairs] + context[pairs:]
                high = context.astype(BF16)
                low = (context - high.astype(F32)).astype(BF16)
                at = slice(head * HEAD_DIM, (head + 1) * HEAD_DIM)
                ctx[:, at] = jnp.concatenate([high, low], axis=0)

    both = jnp.dot(ctx[...], wo[...], preferred_element_type=F32)
    out[0] = both[:pairs] + both[pairs:] + resid[...] * (1.0 / length)


def final_kernel(plan, pooled, left, right):
    rows, n = left.shape[0], pooled.shape[0]
    parts = split3(pooled[...])
    at = lax.broadcasted_iota(jnp.int32, (rows, n), 0)
    for line, out in ((2, left), (3, right)):
        hit = (plan[pl.ds(line, 1), :][:, :n] == at).astype(BF16)
        out[...] = sum(jnp.dot(hit, part, preferred_element_type=F32) for part in parts)


ANY = pl.BlockSpec(memory_space=pl.ANY)
IN_VMEM = pl.BlockSpec(memory_space=pltpu.VMEM)
IN_SMEM = pl.BlockSpec(memory_space=pltpu.SMEM)
LIMIT = pltpu.CompilerParams(vmem_limit_bytes=48 * 1024 * 1024)


def shape(dims, kind):
    return jax.ShapeDtypeStruct(dims, kind)


def qkv(x, first_feature, gain, wq, wk, wv, before, resid, pair_rows):
    rows, wide = x.shape
    block = min(1024, wide)
    start = first_feature // block
    total = wq.shape[1] + wk.shape[1] + wv.shape[1]

    def weight(w):
        return pl.BlockSpec((block, w.shape[1]), lambda i: (i + start, 0))

    whole = lambda dims: pl.BlockSpec(dims, lambda i: (0, 0))
    in_specs = [
        pl.BlockSpec((rows, block), lambda i: (0, i)),
        pl.BlockSpec((1, block), lambda i: (0, i + start)),
        weight(wq),
        weight(wk),
        weight(wv),
    ]
    args = [x, gain, wq, wk, wv]
    if before is not None:
        in_specs += [whole((rows, total)), whole((rows, LANES))]
        args += before
    out_shape = [shape((rows, total), F32), shape((rows, LANES), F32)]
    out_specs = [whole((rows, total)), whole((rows, LANES))]
    if resid:
        out_shape.append(shape((rows // pair_rows, wide), F32))
        out_specs.append(pl.BlockSpec((rows // pair_rows, block), lambda i: (0, i)))
    return pl.pallas_call(
        functools.partial(qkv_kernel, before is None, resid, pair_rows),
        grid=(wide // block,),
        in_specs=in_specs,
        out_specs=out_specs,
        out_shape=out_shape,
        compiler_params=LIMIT,
        cost_estimate=pl.CostEstimate(
            flops=2 * rows * wide * total, bytes_accessed=2 * wide * total, transcendentals=0
        ),
    )(*args)


def on_device(
    left_table,
    right_table,
    left_owner,
    left_row,
    right_owner,
    right_row,
    pair_count,
    norm_gain,
    query_weight,
    key_weight,
    value_weight,
    output_weight,
):
    groups = lax.axis_size("group")
    tensors = lax.axis_size("tensor")
    group, tensor = lax.axis_index("group"), lax.axis_index("tensor")
    pairs_here = left_owner.shape[0]
    rows_here, toks, width = left_table.shape
    share, cap = plan_sizes(groups, pairs_here)
    cells, items = groups * cap, 2 * share
    rows = items * toks
    pair_rows = 2 * toks
    length = pair_rows * tensors
    features = width // tensors
    n = groups * pairs_here

    code = (left_owner[:, 0] * rows_here + left_row) | (
        (right_owner[:, 0] * rows_here + right_row) << RIGHT_SHIFT
    )
    code = jnp.where(jnp.arange(pairs_here, dtype=jnp.int32) < pair_count[0], code, DEAD)
    at = jnp.arange(n, dtype=jnp.int32) // pairs_here
    code = jnp.where(at == group, jnp.tile(code, groups), 0)[None, :]
    codes = lax.all_gather(code, "group", tiled=True)

    half = width // 2
    parts = ((0, half), (half, width - half))
    me = jnp.reshape(group, (1,)).astype(jnp.int32)
    plan, cell_rows = pl.pallas_call(
        functools.partial(plan_kernel, groups, share, cap, rows_here, parts[0][1]),
        in_specs=[IN_SMEM, IN_VMEM, ANY, ANY],
        out_specs=[IN_VMEM, ANY],
        out_shape=[shape((8, LANES), jnp.int32), shape((cells, toks, parts[0][1]), BF16)],
        scratch_shapes=[
            pltpu.SMEM((8, LANES), jnp.int32),
            pltpu.SemaphoreType.DMA(()),
            pltpu.SemaphoreType.DMA((cells,)),
        ],
        compiler_params=LIMIT,
    )(me, codes, left_table, right_table)
    sends = [cell_rows]
    for first, wide in parts[1:]:
        sends.append(
            pl.pallas_call(
                functools.partial(gather_kernel, rows_here, cells, first, wide),
                in_specs=[IN_SMEM, ANY, ANY],
                out_specs=ANY,
                out_shape=shape((cells, toks, wide), BF16),
                scratch_shapes=[pltpu.SemaphoreType.DMA((cells,))],
                compiler_params=LIMIT,
            )(plan, left_table, right_table)
        )
    gain = norm_gain[None, :]
    weights = (query_weight, key_weight, value_weight)
    held = []
    for (first, wide), send in zip(parts, sends):
        got = lax.all_to_all(send, "group", split_axis=0, concat_axis=0, tiled=True)
        held.append(
            pl.pallas_call(
                functools.partial(pick_kernel, items),
                in_specs=[IN_SMEM, ANY],
                out_specs=IN_VMEM,
                out_shape=shape((rows, wide), BF16),
                scratch_shapes=[
                    pltpu.VMEM((items, toks, wide), BF16),
                    pltpu.SemaphoreType.DMA((items,)),
                ],
                compiler_params=LIMIT,
            )(plan, got)
        )

    ring = [(i, (i + 1) % tensors) for i in range(tensors)]
    accs, sqs, resids = [], [], []
    for step in range(tensors):
        before = None
        for (first, wide), x in zip(parts, held):
            out = qkv(x, first, gain, *weights, before, step == 0, pair_rows)
            before = list(out[:2])
            if step == 0:
                resids.append(out[2])
        accs.append(before[0])
        sqs.append(before[1])
        if step < tensors - 1:
            held = [lax.ppermute(x, "tensor", ring) for x in held]
    resid = jnp.concatenate(resids, axis=1)

    block = min(1024, features)
    per = features // block
    total = accs[0].shape[1]
    whole = lambda dims: pl.BlockSpec(dims, lambda i, t: (0, 0))
    partial_sums = pl.pallas_call(
        functools.partial(
            attend_kernel,
            width,
            length,
            pair_rows,
            query_weight.shape[1] // HEAD_DIM,
            key_weight.shape[1] // HEAD_DIM,
        ),
        grid_spec=pltpu.PrefetchScalarGridSpec(
            num_scalar_prefetch=1,
            grid=(width // block,),
            in_specs=[whole((rows, total))] * tensors
            + [whole((rows, LANES))] * tensors
            + [
                pl.BlockSpec((share, block), lambda i, t: (0, i)),
                pl.BlockSpec((output_weight.shape[0], block), lambda i, t: (0, i)),
            ],
            out_specs=pl.BlockSpec(
                (1, share, block), lambda i, t: ((i // per) ^ t[0], 0, i % per)
            ),
            scratch_shapes=[pltpu.VMEM((2 * share, output_weight.shape[0]), BF16)],
        ),
        out_shape=shape((tensors, share, features), F32),
        compiler_params=LIMIT,
        cost_estimate=pl.CostEstimate(
            flops=4 * share * width * output_weight.shape[0],
            bytes_accessed=2 * width * output_weight.shape[0],
            transcendentals=0,
        ),
    )(
        jnp.reshape(tensor, (1,)).astype(jnp.int32), *accs, *sqs, resid, output_weight
    )
    pooled = partial_sums[0]
    for step in range(1, tensors):
        swap = [(i, i ^ step) for i in range(tensors)]
        pooled = pooled + lax.ppermute(partial_sums[step], "tensor", swap)
    everyone = lax.all_gather(pooled, "group", tiled=True)

    def fast():
        return tuple(
            pl.pallas_call(
                final_kernel,
                in_specs=[IN_VMEM, IN_VMEM],
                out_specs=[IN_VMEM, IN_VMEM],
                out_shape=[shape((rows_here, features), F32)] * 2,
                compiler_params=LIMIT,
            )(plan, everyone)
        )

    def general():
        return general_program(
            left_table,
            right_table,
            left_owner,
            left_row,
            right_owner,
            right_row,
            pair_count,
            norm_gain,
            query_weight,
            key_weight,
            value_weight,
            output_weight,
        )

    return lax.cond(plan[4, 0] > 0, general, fast)


def solution(mesh):
    return jax.shard_map(
        on_device,
        mesh=mesh,
        in_specs=(
            P("group", "tensor", None),
            P("group", "tensor", None),
            P("group", None),
            P("group"),
            P("group", None),
            P("group"),
            P("group"),
            P(),
            P(None, "tensor"),
            P(None, "tensor"),
            P(None, "tensor"),
            P("tensor", None),
        ),
        out_specs=(P("group", "tensor"), P("group", "tensor")),
        check_vma=False,
    )
```

```python
import functools

import jax
import jax.numpy as jnp
from jax import lax
from jax.experimental import pallas as pl
from jax.experimental.pallas import tpu as pltpu
from jax.sharding import PartitionSpec as P

HEAD_DIM = 128


score_scale = 4.0


def slot_plan(owner, groups, capacity):
    count = owner.shape[0]
    order = jnp.arange(count, dtype=jnp.int32)
    same_owner = owner[:, None] == owner[None, :]
    earlier = order[None, :] < order[:, None]
    rank = jnp.sum(jnp.logical_and(same_owner, earlier), axis=1)
    owner_hit = owner[:, None, None] == jnp.arange(groups, dtype=jnp.int32)[None, :, None]
    rank_hit = rank[:, None, None] == jnp.arange(capacity, dtype=jnp.int32)[None, None, :]
    return (rank, jnp.logical_and(owner_hit, rank_hit))


def request_ids(slot_match, row_index):
    return jnp.sum(jnp.where(slot_match, row_index[:, None, None], 0), axis=0)


def owner_sums(row_ids, arrived, rows_here):
    onehot = (row_ids[:, :, None] == jnp.arange(rows_here, dtype=jnp.int32)[None, None, :]).astype(
        jnp.float32
    )
    return jnp.einsum("gcr,gcf->rf", onehot, arrived, precision=lax.Precision.HIGHEST)


def general_program(
    left_table,
    right_table,
    left_owner,
    left_row,
    right_owner,
    right_row,
    pair_count,
    norm_gain,
    query_weight,
    key_weight,
    value_weight,
    output_weight,
):
    groups = lax.axis_size("group")
    tensors = lax.axis_size("tensor")
    pairs_here = left_owner.shape[0]
    capacity = 2 * pairs_here // groups
    rows_here = left_table.shape[0]
    width = left_table.shape[2]
    feature_share = width // tensors
    left_group = left_owner[:, 0]
    right_group = right_owner[:, 0]
    left_rank, left_match = slot_plan(left_group, groups, capacity)
    right_rank, right_match = slot_plan(right_group, groups, capacity)
    left_request = request_ids(left_match, left_row)
    right_request = request_ids(right_match, right_row)
    left_spread = jnp.broadcast_to(left_request[:, None, :], (groups, tensors, capacity)).reshape(
        groups * tensors, capacity
    )
    right_spread = jnp.broadcast_to(right_request[:, None, :], (groups, tensors, capacity)).reshape(
        groups * tensors, capacity
    )
    left_wanted, right_wanted = (
        lax.all_to_all(left_spread, ("group", "tensor"), split_axis=0, concat_axis=0, tiled=True),
        lax.all_to_all(right_spread, ("group", "tensor"), split_axis=0, concat_axis=0, tiled=True),
    )
    left_back, right_back = (
        lax.all_to_all(
            left_table[left_wanted], ("group", "tensor"), split_axis=0, concat_axis=0, tiled=True
        ),
        lax.all_to_all(
            right_table[right_wanted], ("group", "tensor"), split_axis=0, concat_axis=0, tiled=True
        ),
    )
    left_back = left_back.reshape(groups, tensors, capacity, left_table.shape[1], width)
    right_back = right_back.reshape(groups, tensors, capacity, right_table.shape[1], width)
    left_tokens = left_back[left_group, :, left_rank].reshape(
        pairs_here, tensors * left_table.shape[1], width
    )
    right_tokens = right_back[right_group, :, right_rank].reshape(
        pairs_here, tensors * right_table.shape[1], width
    )
    left_owned = left_wanted.reshape(groups, tensors, capacity)[:, 0]
    right_owned = right_wanted.reshape(groups, tensors, capacity)[:, 0]
    inputs = jnp.concatenate([left_tokens, right_tokens], axis=1)
    length = inputs.shape[1]
    flat = inputs.reshape(pairs_here * length, width)
    wide = flat.astype(jnp.float32)
    scale = lax.rsqrt(jnp.mean(wide * wide, axis=-1, keepdims=True) + 1e-05)
    normed = (wide * scale * norm_gain[None, :]).astype(jnp.bfloat16)
    q_raw = jnp.dot(normed, query_weight, preferred_element_type=jnp.float32)
    k_raw = jnp.dot(normed, key_weight, preferred_element_type=jnp.float32)
    values = jnp.dot(normed, value_weight, preferred_element_type=jnp.float32).astype(jnp.bfloat16)
    kv_local = key_weight.shape[1] // HEAD_DIM
    share = query_weight.shape[1] // HEAD_DIM // kv_local
    q_heads = q_raw.reshape(pairs_here * length, kv_local * share, HEAD_DIM)
    k_heads = k_raw.reshape(pairs_here * length, kv_local, HEAD_DIM)
    q_norm = (
        q_heads * lax.rsqrt(jnp.mean(q_heads * q_heads, axis=-1, keepdims=True) + 1e-06)
    ).astype(jnp.bfloat16)
    k_norm = (
        k_heads * lax.rsqrt(jnp.mean(k_heads * k_heads, axis=-1, keepdims=True) + 1e-06)
    ).astype(jnp.bfloat16)
    q_five = q_norm.reshape(pairs_here, length, kv_local, share, HEAD_DIM)
    k_four = k_norm.reshape(pairs_here, length, kv_local, HEAD_DIM)
    v_four = values.reshape(pairs_here, length, kv_local, HEAD_DIM)
    scores = jnp.einsum("pqkgd,pskd->pkgqs", q_five, k_four, preferred_element_type=jnp.float32) * (
        score_scale / HEAD_DIM
    )
    expo = jnp.exp(scores)
    weights = (expo / jnp.sum(expo, axis=-1, keepdims=True)).astype(jnp.bfloat16)
    context = jnp.einsum(
        "pkgqs,pskd->pqkgd", weights, v_four, preferred_element_type=jnp.float32
    ).astype(jnp.bfloat16)
    context = context.reshape(pairs_here * length, kv_local * share * HEAD_DIM)
    attended = jnp.dot(context, output_weight, preferred_element_type=jnp.float32)
    head_term = jnp.mean(attended.reshape(pairs_here, length, width), axis=1)
    head_part = lax.psum_scatter(head_term, "tensor", scatter_dimension=1, tiled=True)
    feature_start = lax.axis_index("tensor") * feature_share
    own_features = lax.dynamic_slice_in_dim(inputs, feature_start, feature_share, 2)
    residual_mean = jnp.mean(own_features.astype(jnp.float32), axis=1)
    live = jnp.arange(pairs_here, dtype=jnp.int32) < pair_count[0]
    pooled = jnp.where(live[:, None], residual_mean + head_part, jnp.zeros_like(head_part))
    left_send = jnp.einsum(
        "pgc,pf->gcf", left_match.astype(jnp.float32), pooled, precision=lax.Precision.HIGHEST
    )
    right_send = jnp.einsum(
        "pgc,pf->gcf", right_match.astype(jnp.float32), pooled, precision=lax.Precision.HIGHEST
    )
    left_got, right_got = (
        lax.all_to_all(left_send, "group", split_axis=0, concat_axis=0, tiled=True),
        lax.all_to_all(right_send, "group", split_axis=0, concat_axis=0, tiled=True),
    )
    left_sums = owner_sums(left_owned, left_got, rows_here)
    right_sums = owner_sums(right_owned, right_got, rows_here)
    return (left_sums, right_sums)

LANES = 128
DEAD = -1
RIGHT_SHIFT = 12
DEALS = (43, 21, 34, 1, 15, 10, 61, 5, 7, 50, 11, 4)
LOADS = 8
COST = 512
WO_PARTS = 2
BF16 = jnp.bfloat16
F32 = jnp.float32


def log2(number):
    bits = number.bit_length() - 1
    assert 1 << bits == number
    return bits


def plan_sizes(groups, pairs_here):
    share = pairs_here // 2
    mean = -(-2 * share // groups)
    return (share, min(LANES // groups, (5 * mean + 1) // 2))


def column(row):
    n = row.shape[1]
    return jnp.transpose(jnp.broadcast_to(row, (n, n)))[:, :1]


def split3(wide):
    high = wide.astype(BF16)
    rest = wide - high.astype(F32)
    mid = rest.astype(BF16)
    low = (rest - mid.astype(F32)).astype(BF16)
    return (high, mid, low)


def plan_body(codes, me, groups, share, cap, rows_here):
    n = codes.shape[1]
    gbits, rbits = log2(groups), log2(rows_here)
    live_total = groups * share
    live = codes >= 0
    left = jnp.where(live, codes & ((1 << RIGHT_SHIFT) - 1), 0)
    right = jnp.where(live, codes >> RIGHT_SHIFT, 0)
    left_own, right_own = left >> rbits, right >> rbits
    order = lax.broadcasted_iota(jnp.int32, (1, n), 1)
    owners = lax.broadcasted_iota(jnp.int32, (groups, n), 0)
    load_of = (left_own == owners).astype(F32) + (right_own == owners).astype(F32)
    load_of = jnp.where(live, load_of, 0.0).astype(BF16)
    live_c, left_c, right_c = column(live.astype(jnp.int32)), column(left), column(right)
    lo_c, ro_c = left_c >> rbits, right_c >> rbits
    order_c = lax.broadcasted_iota(jnp.int32, (n, 1), 0)

    def key(one, other, alive, at, deal):
        major, minor = (other, one) if deal >> 5 else (one, other)
        minor = (minor * (2 * ((deal >> 3) & 3) + 1) + (deal & 7) * major) & (groups - 1)
        return jnp.where(alive, ((major << gbits) + minor) * n, groups * groups * n) + at

    best, best_load = None, None
    for deal in DEALS:
        key_r = key(left_own, right_own, live, order, deal)
        key_c = key(lo_c, ro_c, live_c > 0, order_c, deal)
        rank = jnp.sum((key_c < key_r).astype(jnp.int32), axis=0, keepdims=True)
        to = jnp.where(rank < live_total, rank & (groups - 1), groups)
        hit = (to == owners).astype(BF16)
        load = lax.dot_general(hit, load_of, (((1,), (1,)), ((), ())), preferred_element_type=F32)
        most = jnp.max(jnp.max(load, axis=1, keepdims=True), axis=0, keepdims=True)
        if best is None:
            best, best_load = rank, most
        else:
            better = most < best_load
            best = jnp.where(better, rank, best)
            best_load = jnp.where(better, most, best_load)
    rank = best
    rank_c = column(rank)
    to_c = jnp.where(rank_c < live_total, rank_c & (groups - 1), groups)
    slot_c = rank_c >> gbits
    to = jnp.where(rank < live_total, rank & (groups - 1), groups)
    same_to = to_c == to
    earlier = jnp.logical_and(same_to, rank < rank_c)

    def count(mask):
        return jnp.sum(mask.astype(jnp.int32), axis=1, keepdims=True)

    left_pos = count(jnp.logical_and(earlier, lo_c == left_own))
    right_pos = count(jnp.logical_and(earlier, ro_c == right_own)) + count(
        jnp.logical_and(jnp.logical_and(same_to, rank < live_total), ro_c == left_own)
    )
    lane = lax.broadcasted_iota(jnp.int32, (n, LANES), 1)
    alive = rank_c < live_total

    def place(mask, at, value):
        return jnp.sum(
            jnp.where(jnp.logical_and(mask, at == lane), value, 0), axis=0, keepdims=True
        )

    left_in = jnp.logical_and(alive, left_pos < cap)
    right_in = jnp.logical_and(alive, right_pos < cap)
    local_left, local_right = left_c & (rows_here - 1), right_c & (rows_here - 1)
    send = place(
        jnp.logical_and(left_in, lo_c == me), to_c * cap + left_pos, local_left + 1
    ) + place(
        jnp.logical_and(right_in, ro_c == me), to_c * cap + right_pos, local_right + rows_here + 1
    )
    mine = jnp.logical_and(alive, to_c == me)
    fetch = place(
        jnp.logical_and(mine, left_in), slot_c * 2, lo_c * cap + left_pos
    ) + place(jnp.logical_and(mine, right_in), slot_c * 2 + 1, ro_c * cap + right_pos)
    back = to_c * share + slot_c
    left_row = place(jnp.logical_and(alive, lo_c == me), back, local_left + 1) - 1
    right_row = place(jnp.logical_and(alive, ro_c == me), back, local_right + 1) - 1
    over = jnp.broadcast_to((best_load > cap).astype(jnp.int32), (1, LANES))
    return (send, fetch, left_row, right_row, over)


def gather_cells(plan, left, right, out, sems, rows_here, cells, first, wide):
    def begin(cell, carry):
        index = plan[0, cell] - 1
        row = index & (rows_here - 1)
        for side, table in ((0, left), (1, right)):

            @pl.when(jnp.logical_and(index >= side * rows_here, index < (side + 1) * rows_here))
            def _():
                pltpu.make_async_copy(
                    table.at[row, :, pl.ds(first, wide)], out.at[cell], sems.at[cell]
                ).start()

        return carry

    def finish(cell, carry):
        @pl.when(plan[0, cell] > 0)
        def _():
            pltpu.make_async_copy(
                left.at[0, :, pl.ds(first, wide)], out.at[cell], sems.at[cell]
            ).wait()

        return carry

    lax.fori_loop(0, cells, begin, 0)
    lax.fori_loop(0, cells, finish, 0)


def plan_kernel(groups, share, cap, rows_here, wide, me, codes, left, right, plan_out, out, plan, sem, sems):
    rows = jnp.sum(codes[...], axis=0, keepdims=True)
    table = plan_body(rows, me[0], groups, share, cap, rows_here)
    for at, row in enumerate(table):
        plan_out[pl.ds(at, 1), :] = row
    copy = pltpu.make_async_copy(plan_out, plan, sem)
    copy.start()
    copy.wait()
    gather_cells(plan, left, right, out, sems, rows_here, groups * cap, 0, wide)


def gather_kernel(rows_here, cells, first, wide, plan, left, right, out, sems):
    gather_cells(plan, left, right, out, sems, rows_here, cells, first, wide)


def pick_kernel(items, after, plan, got, *refs):
    out, held, sems = refs[after:]

    def begin(item, carry):
        pltpu.make_async_copy(got.at[plan[1, item]], held.at[item], sems.at[item]).start()
        return carry

    def finish(item, carry):
        pltpu.make_async_copy(got.at[0], held.at[item], sems.at[item]).wait()
        return carry

    lax.fori_loop(0, items, begin, 0)
    lax.fori_loop(0, items, finish, 0)
    out[...] = held[...].reshape(out.shape)


def products(x_refs, gain, weights, first, ready=None):
    rows, wide = sum(x.shape[0] for x in x_refs), x_refs[0].shape[1]
    block = wide // LOADS
    widths = [w.shape[1] for w in weights]

    def one(i, carry):
        sums, square = carry
        if ready is not None:
            ready(i)
        at = pl.multiple_of(i * block, block)
        x = jnp.concatenate([x[:, pl.ds(at, block)] for x in x_refs], axis=0).astype(F32)
        normed = (x * gain[:, pl.ds(first + at, block)]).astype(BF16)
        sums = tuple(
            total + jnp.dot(normed, w[pl.ds(at, block), :], preferred_element_type=F32)
            for total, w in zip(sums, weights)
        )
        return (sums, square + jnp.sum(x * x, axis=1, keepdims=True))

    zero = (tuple(jnp.zeros((rows, n), F32) for n in widths), jnp.zeros((rows, 1), F32))
    sums, square = lax.fori_loop(0, LOADS, one, zero)
    return (jnp.concatenate(sums, axis=1), square)


def qkv_kernel(shards, first, loads, keep, extra, more, resid, after, pair_rows, *refs):
    refs = list(refs)
    x_refs = [refs.pop(0) for _ in range(shards)]
    gain = refs.pop(0)
    sources = [refs.pop(0) for _ in range(3)]
    before = [refs.pop(0) for _ in range(2)] if more else None
    extra_source = refs.pop(0) if extra is not None else None
    del refs[:after]
    sums_out, square_out = refs.pop(0), refs.pop(0)
    resid_out = refs.pop(0) if resid else None
    ready, weights = None, sources
    if keep:
        weights = [refs.pop(0) for _ in range(3)]
    extra_held = refs.pop(0) if extra is not None else None
    if loads and not keep:
        weights = [refs.pop(0) for _ in range(3)]
    if loads:
        sems = refs.pop(0)
        block = x_refs[0].shape[1] // LOADS

        def copy(which, i):
            at = i * block
            return pltpu.make_async_copy(
                sources[which].at[pl.ds(first + at, block)],
                weights[which].at[pl.ds(at, block)],
                sems.at[which, i],
            )

        for i in range(LOADS):
            for which in range(3):
                copy(which, i).start()

        def ready(i):
            for which in range(3):
                copy(which, i).wait()

    if extra is not None:
        extra_copy = pltpu.make_async_copy(
            extra_source.at[pl.ds(extra, extra_held.shape[0])], extra_held, refs.pop(0)
        )
        extra_copy.start()
    sums, square = products(x_refs, gain, weights, first, ready)
    square = jnp.broadcast_to(square, (square.shape[0], LANES))
    if more:
        sums += before[0][...]
        square += before[1][...]
    sums_out[...] = sums
    square_out[...] = square
    if resid:
        rows = x_refs[0].shape[0]
        pairs = rows // pair_rows
        pair = lax.broadcasted_iota(jnp.int32, (pairs, rows), 1) // pair_rows
        mine = (pair == lax.broadcasted_iota(jnp.int32, (pairs, rows), 0)).astype(BF16)
        resid_out[...] = jnp.dot(mine, x_refs[0][...], preferred_element_type=F32)
    if extra is not None:
        extra_copy.wait()


def tail_kernel(
    shards, groups, parts, width, length, pair_rows, first, t_ref, x_ref, gain, wq, wk, wv, *refs
):
    wos, refs = refs[:WO_PARTS], refs[WO_PARTS:]
    accs, sqs, resids = refs[:groups], refs[groups : 2 * groups], refs[2 * groups : 2 * groups + parts]
    out, ctx = refs[2 * groups + parts :]
    pairs, features = out.shape[1:]
    heads, kv_heads = wq.shape[1] // HEAD_DIM, wk.shape[1] // HEAD_DIM
    share = heads // kv_heads
    sums, square = products([x_ref], gain, (wq, wk, wv), first)
    acc = jnp.concatenate([a[...] for a in accs[:-1]] + [accs[-1][...] + sums], axis=0)
    sq = jnp.concatenate([s[:, :1] for s in sqs[:-1]] + [sqs[-1][:, :1] + square], axis=0)
    tokens = acc.shape[0]
    acc = acc * lax.rsqrt(sq * (1.0 / width) + 1e-05)
    rows = tokens // shards
    row = lax.broadcasted_iota(jnp.int32, (share * tokens, tokens), 0)
    col = lax.broadcasted_iota(jnp.int32, (share * tokens, tokens), 1)
    same = ((row & (rows - 1)) >> log2(pair_rows)) == ((col & (rows - 1)) >> log2(pair_rows))
    pair = lax.broadcasted_iota(jnp.int32, (pairs, tokens), 0)
    token = lax.broadcasted_iota(jnp.int32, (pairs, tokens), 1)
    member = ((token & (rows - 1)) >> log2(pair_rows)) == pair
    nq, nk = heads * HEAD_DIM, kv_heads * HEAD_DIM

    def unit(part):
        return (part * lax.rsqrt(jnp.mean(part * part, axis=1, keepdims=True) + 1e-06)).astype(
            BF16
        )

    def head(start):
        return acc[:, start : start + HEAD_DIM]

    for kv in range(kv_heads):
        k = unit(head(nq + kv * HEAD_DIM))
        v = head(nq + nk + kv * HEAD_DIM).astype(BF16)
        q = jnp.concatenate(
            [unit(head((kv * share + i) * HEAD_DIM)) for i in range(share)], axis=0
        )
        scores = lax.dot_general(
            q, k, (((1,), (1,)), ((), ())), preferred_element_type=F32
        ) * (score_scale / HEAD_DIM)
        expo = jnp.where(same, jnp.exp(scores), 0.0)
        weights = expo / jnp.sum(expo, axis=1, keepdims=True)
        spread = []
        for i in range(share):
            mean = jnp.sum(weights[i * tokens : (i + 1) * tokens], axis=0, keepdims=True)
            spread.append(jnp.where(member, mean * (1.0 / length), 0.0))
        spread = jnp.concatenate(spread, axis=0)
        high = spread.astype(BF16)
        low = (spread - high.astype(F32)).astype(BF16)
        context = jnp.dot(
            jnp.concatenate([high, low], axis=0), v, preferred_element_type=F32
        )
        context = context[: share * pairs] + context[share * pairs :]
        for i in range(share):
            one_head = context[i * pairs : (i + 1) * pairs]
            high = one_head.astype(BF16)
            low = (one_head - high.astype(F32)).astype(BF16)
            at = (kv * share + i) * HEAD_DIM
            ctx[:, at : at + HEAD_DIM] = jnp.concatenate([high, low], axis=0)

    block = min(512, features)
    per = features // block
    done = 0
    for resid in resids:

        def one(i, carry):
            here = pl.multiple_of(i * block, block)
            i = i + done // block
            at = pl.multiple_of(i * block, block)
            deep = wos[0].shape[0]
            both = sum(
                jnp.dot(
                    ctx[:, j * deep : (j + 1) * deep],
                    wo[:, pl.ds(at, block)],
                    preferred_element_type=F32,
                )
                for j, wo in enumerate(wos)
            )
            both = both[:pairs] + both[pairs:] + resid[:, pl.ds(here, block)] * (1.0 / length)
            inside = pl.multiple_of((i % per) * block, block)
            out[pl.ds((i // per) ^ t_ref[0], 1), :, pl.ds(inside, block)] = both[None]
            return carry

        lax.fori_loop(0, resid.shape[1] // block, one, 0)
        done += resid.shape[1]


def final_kernel(plan, pooled, left, right):
    rows, n = left.shape[0], pooled.shape[0]
    parts = split3(pooled[...])
    at = lax.broadcasted_iota(jnp.int32, (rows, n), 0)
    for line, out in ((2, left), (3, right)):
        hit = (plan[pl.ds(line, 1), :][:, :n] == at).astype(BF16)
        out[...] = sum(jnp.dot(hit, part, preferred_element_type=F32) for part in parts)


ANY = pl.BlockSpec(memory_space=pl.ANY)
IN_VMEM = pl.BlockSpec(memory_space=pltpu.VMEM)
IN_SMEM = pl.BlockSpec(memory_space=pltpu.SMEM)
LIMIT = pltpu.CompilerParams(vmem_limit_bytes=6 * 1024 * 1024)
WIDE_LIMIT = pltpu.CompilerParams(vmem_limit_bytes=24 * 1024 * 1024)


def shape(dims, kind):
    return jax.ShapeDtypeStruct(dims, kind)


def held_in_vmem(array):
    return pltpu.with_memory_space_constraint(array, pltpu.VMEM)


def qkv(xs, first, gain, weights, loads, keep, before, resid, pair_rows, extra=None, after=()):
    rows, wide = sum(x.shape[0] for x in xs), xs[0].shape[1]
    total = sum(w.shape[1] for w in weights)
    args = [*xs, gain, *weights] + (before or [])
    in_specs = [IN_VMEM] * (len(xs) + 1) + [ANY if loads else IN_VMEM] * 3
    in_specs += [IN_VMEM] * len(before or [])
    out_shape = [shape((rows, total), F32), shape((rows, LANES), F32)]
    scratch = []
    if resid:
        out_shape.append(shape((xs[0].shape[0] // pair_rows, wide), F32))
    if loads:
        halves = [pltpu.VMEM((wide, w.shape[1]), w.dtype) for w in weights]
        if keep:
            out_shape += halves
        else:
            scratch += halves
        scratch.append(pltpu.SemaphoreType.DMA((3, LOADS)))
    if extra is not None:
        array, part, at = extra
        args.append(array)
        in_specs.append(ANY)
        out_shape.append(pltpu.VMEM((part, array.shape[1]), array.dtype))
        scratch.append(pltpu.SemaphoreType.DMA(()))
    args += after
    in_specs += [ANY] * len(after)
    out = pl.pallas_call(
        functools.partial(
            qkv_kernel,
            len(xs),
            first,
            loads,
            keep,
            None if extra is None else extra[2],
            before is not None,
            resid,
            len(after),
            pair_rows,
        ),
        in_specs=in_specs,
        out_specs=[IN_VMEM] * len(out_shape),
        out_shape=out_shape,
        scratch_shapes=scratch,
        compiler_params=LIMIT if keep or not loads else WIDE_LIMIT,
        cost_estimate=pl.CostEstimate(
            flops=COST * wide * total, bytes_accessed=2 * rows * wide, transcendentals=0
        ),
    )(*args)
    out = list(out)
    result = {"sums": [out.pop(0), out.pop(0)]}
    if resid:
        result["resid"] = out.pop(0)
    if keep:
        result["weights"] = [held_in_vmem(out.pop(0)) for _ in range(3)]
    if extra is not None:
        result["extra"] = held_in_vmem(out.pop(0))
    return result


def on_device(
    left_table,
    right_table,
    left_owner,
    left_row,
    right_owner,
    right_row,
    pair_count,
    norm_gain,
    query_weight,
    key_weight,
    value_weight,
    output_weight,
):
    groups = lax.axis_size("group")
    tensors = lax.axis_size("tensor")
    group, tensor = lax.axis_index("group"), lax.axis_index("tensor")
    pairs_here = left_owner.shape[0]
    rows_here, toks, width = left_table.shape
    share, cap = plan_sizes(groups, pairs_here)
    cells, items = groups * cap, 2 * share
    rows = items * toks
    pair_rows = 2 * toks
    length = pair_rows * tensors
    features = width // tensors
    n = groups * pairs_here

    code = (left_owner[:, 0] * rows_here + left_row) | (
        (right_owner[:, 0] * rows_here + right_row) << RIGHT_SHIFT
    )
    code = jnp.where(jnp.arange(pairs_here, dtype=jnp.int32) < pair_count[0], code, DEAD)
    at = jnp.arange(n, dtype=jnp.int32) // pairs_here
    code = jnp.where(at == group, jnp.tile(code, groups), 0)[None, :]
    codes = lax.all_gather(code, "group", tiled=True)

    head = width * 5 // 8
    parts = ((0, head), (head, width - head))
    me = jnp.reshape(group, (1,)).astype(jnp.int32)
    plan, cell_rows = pl.pallas_call(
        functools.partial(plan_kernel, groups, share, cap, rows_here, parts[0][1]),
        in_specs=[IN_SMEM, IN_VMEM, ANY, ANY],
        out_specs=[IN_VMEM, IN_VMEM],
        out_shape=[shape((8, LANES), jnp.int32), shape((cells, toks, parts[0][1]), BF16)],
        scratch_shapes=[
            pltpu.SMEM((8, LANES), jnp.int32),
            pltpu.SemaphoreType.DMA(()),
            pltpu.SemaphoreType.DMA((cells,)),
        ],
        compiler_params=LIMIT,
    )(me, codes, left_table, right_table)
    sends = [cell_rows]
    for first, wide in parts[1:]:
        sends.append(
            pl.pallas_call(
                functools.partial(gather_kernel, rows_here, cells, first, wide),
                in_specs=[IN_SMEM, ANY, ANY],
                out_specs=IN_VMEM,
                out_shape=shape((cells, toks, wide), BF16),
                scratch_shapes=[pltpu.SemaphoreType.DMA((cells,))],
                compiler_params=LIMIT,
            )(plan, left_table, right_table)
        )
    gain = norm_gain[None, :]
    weights = (query_weight, key_weight, value_weight)
    ring = [(i, (i + 1) % tensors) for i in range(tensors)]

    def exchange(send):
        return lax.all_to_all(send, "group", split_axis=0, concat_axis=0, tiled=True)

    def pick(got, after):
        wide = got.shape[2]
        return pl.pallas_call(
            functools.partial(pick_kernel, items, len(after)),
            in_specs=[IN_SMEM, ANY] + [ANY] * len(after),
            out_specs=IN_VMEM,
            out_shape=shape((rows, wide), BF16),
            scratch_shapes=[
                pltpu.VMEM((items, toks, wide), BF16),
                pltpu.SemaphoreType.DMA((items,)),
            ],
            compiler_params=LIMIT,
        )(plan, got, *after)

    def pass_on(x):
        return lax.ppermute(x, "tensor", ring)

    one, two = [[pick(exchange(sends[0]), [])], []]
    first = qkv(one, parts[0][0], gain, weights, True, False, None, True, pair_rows)
    one.append(pass_on(one[0]))
    two.append(pick(exchange(sends[1]), [first["sums"][1], one[1]]))
    for _ in range(2, tensors):
        one.append(pass_on(one[-1]))
    for _ in range(1, tensors):
        two.append(pass_on(two[-1]))
    shards = [(0, 1), (1, 3)] + [(i, i + 1) for i in range(3, tensors)]
    deep = output_weight.shape[0] // WO_PARTS
    sums, wos, held_one, held_two = [first["sums"]], [], None, None
    for low, high in shards[1:]:
        out = qkv(
            one[low:high],
            parts[0][0],
            gain,
            held_one or weights,
            held_one is None,
            held_one is None,
            None,
            False,
            pair_rows,
            (output_weight, deep, 0) if low == 3 else None,
            [two[0]] if held_one is None else [],
        )
        held_one = held_one or out["weights"]
        sums.append(out["sums"])
        if "extra" in out:
            wos.append(out["extra"])
    resids = [first["resid"]]
    for at, (low, high) in enumerate(shards[:-1]):
        out = qkv(
            two[low:high],
            parts[1][0],
            gain,
            held_two or weights,
            held_two is None,
            held_two is None,
            sums[at],
            low == 0,
            pair_rows,
            (output_weight, deep, deep) if low == 1 else None,
        )
        held_two = held_two or out["weights"]
        sums[at] = out["sums"]
        if low == 0:
            resids.append(out["resid"])
        if "extra" in out:
            wos.append(out["extra"])
    held, held_weights = two, [held_two]
    accs, sqs = [s[0] for s in sums], [s[1] for s in sums]

    args = [held[-1], gain, *held_weights[-1], *wos, *accs, *sqs, *resids]
    partial_sums = pl.pallas_call(
        functools.partial(
            tail_kernel, tensors, len(shards), len(parts), width, length, pair_rows, parts[-1][0]
        ),
        in_specs=[IN_SMEM] + [IN_VMEM] * len(args),
        out_specs=IN_VMEM,
        out_shape=shape((tensors, share, features), F32),
        scratch_shapes=[pltpu.VMEM((2 * share, output_weight.shape[0]), BF16)],
        compiler_params=LIMIT,
        cost_estimate=pl.CostEstimate(
            flops=32 * share * width * output_weight.shape[0],
            bytes_accessed=2 * rows * width,
            transcendentals=0,
        ),
    )(jnp.reshape(tensor, (1,)).astype(jnp.int32), *args)
    pooled = partial_sums[0]
    for step in range(1, tensors):
        swap = [(i, i ^ step) for i in range(tensors)]
        pooled = pooled + lax.ppermute(partial_sums[step], "tensor", swap)
    everyone = lax.all_gather(pooled, "group", tiled=True)

    def fast():
        return tuple(
            pl.pallas_call(
                final_kernel,
                in_specs=[IN_VMEM, IN_VMEM],
                out_specs=[IN_VMEM, IN_VMEM],
                out_shape=[shape((rows_here, features), F32)] * 2,
                compiler_params=LIMIT,
            )(plan, everyone)
        )

    def general():
        return general_program(
            left_table,
            right_table,
            left_owner,
            left_row,
            right_owner,
            right_row,
            pair_count,
            norm_gain,
            query_weight,
            key_weight,
            value_weight,
            output_weight,
        )

    return lax.cond(plan[4, 0] > 0, general, fast)


def solution(mesh):
    return jax.shard_map(
        on_device,
        mesh=mesh,
        in_specs=(
            P("group", "tensor", None),
            P("group", "tensor", None),
            P("group", None),
            P("group"),
            P("group", None),
            P("group"),
            P("group"),
            P(),
            P(None, "tensor"),
            P(None, "tensor"),
            P(None, "tensor"),
            P("tensor", None),
        ),
        out_specs=(P("group", "tensor"), P("group", "tensor")),
        check_vma=False,
    )
```

```python
import functools

import jax
import jax.numpy as jnp
from jax import lax
from jax.experimental import pallas as pl
from jax.experimental.pallas import tpu as pltpu
from jax.sharding import PartitionSpec as P

HEAD_DIM = 128


score_scale = 4.0


def slot_plan(owner, groups, capacity):
    count = owner.shape[0]
    order = jnp.arange(count, dtype=jnp.int32)
    same_owner = owner[:, None] == owner[None, :]
    earlier = order[None, :] < order[:, None]
    rank = jnp.sum(jnp.logical_and(same_owner, earlier), axis=1)
    owner_hit = owner[:, None, None] == jnp.arange(groups, dtype=jnp.int32)[None, :, None]
    rank_hit = rank[:, None, None] == jnp.arange(capacity, dtype=jnp.int32)[None, None, :]
    return (rank, jnp.logical_and(owner_hit, rank_hit))


def request_ids(slot_match, row_index):
    return jnp.sum(jnp.where(slot_match, row_index[:, None, None], 0), axis=0)


def owner_sums(row_ids, arrived, rows_here):
    onehot = (row_ids[:, :, None] == jnp.arange(rows_here, dtype=jnp.int32)[None, None, :]).astype(
        jnp.float32
    )
    return jnp.einsum("gcr,gcf->rf", onehot, arrived, precision=lax.Precision.HIGHEST)


def general_program(
    left_table,
    right_table,
    left_owner,
    left_row,
    right_owner,
    right_row,
    pair_count,
    norm_gain,
    query_weight,
    key_weight,
    value_weight,
    output_weight,
):
    groups = lax.axis_size("group")
    tensors = lax.axis_size("tensor")
    pairs_here = left_owner.shape[0]
    capacity = 2 * pairs_here // groups
    rows_here = left_table.shape[0]
    width = left_table.shape[2]
    feature_share = width // tensors
    left_group = left_owner[:, 0]
    right_group = right_owner[:, 0]
    left_rank, left_match = slot_plan(left_group, groups, capacity)
    right_rank, right_match = slot_plan(right_group, groups, capacity)
    left_request = request_ids(left_match, left_row)
    right_request = request_ids(right_match, right_row)
    left_spread = jnp.broadcast_to(left_request[:, None, :], (groups, tensors, capacity)).reshape(
        groups * tensors, capacity
    )
    right_spread = jnp.broadcast_to(right_request[:, None, :], (groups, tensors, capacity)).reshape(
        groups * tensors, capacity
    )
    left_wanted, right_wanted = (
        lax.all_to_all(left_spread, ("group", "tensor"), split_axis=0, concat_axis=0, tiled=True),
        lax.all_to_all(right_spread, ("group", "tensor"), split_axis=0, concat_axis=0, tiled=True),
    )
    left_back, right_back = (
        lax.all_to_all(
            left_table[left_wanted], ("group", "tensor"), split_axis=0, concat_axis=0, tiled=True
        ),
        lax.all_to_all(
            right_table[right_wanted], ("group", "tensor"), split_axis=0, concat_axis=0, tiled=True
        ),
    )
    left_back = left_back.reshape(groups, tensors, capacity, left_table.shape[1], width)
    right_back = right_back.reshape(groups, tensors, capacity, right_table.shape[1], width)
    left_tokens = left_back[left_group, :, left_rank].reshape(
        pairs_here, tensors * left_table.shape[1], width
    )
    right_tokens = right_back[right_group, :, right_rank].reshape(
        pairs_here, tensors * right_table.shape[1], width
    )
    left_owned = left_wanted.reshape(groups, tensors, capacity)[:, 0]
    right_owned = right_wanted.reshape(groups, tensors, capacity)[:, 0]
    inputs = jnp.concatenate([left_tokens, right_tokens], axis=1)
    length = inputs.shape[1]
    flat = inputs.reshape(pairs_here * length, width)
    wide = flat.astype(jnp.float32)
    scale = lax.rsqrt(jnp.mean(wide * wide, axis=-1, keepdims=True) + 1e-05)
    normed = (wide * scale * norm_gain[None, :]).astype(jnp.bfloat16)
    q_raw = jnp.dot(normed, query_weight, preferred_element_type=jnp.float32)
    k_raw = jnp.dot(normed, key_weight, preferred_element_type=jnp.float32)
    values = jnp.dot(normed, value_weight, preferred_element_type=jnp.float32).astype(jnp.bfloat16)
    kv_local = key_weight.shape[1] // HEAD_DIM
    share = query_weight.shape[1] // HEAD_DIM // kv_local
    q_heads = q_raw.reshape(pairs_here * length, kv_local * share, HEAD_DIM)
    k_heads = k_raw.reshape(pairs_here * length, kv_local, HEAD_DIM)
    q_norm = (
        q_heads * lax.rsqrt(jnp.mean(q_heads * q_heads, axis=-1, keepdims=True) + 1e-06)
    ).astype(jnp.bfloat16)
    k_norm = (
        k_heads * lax.rsqrt(jnp.mean(k_heads * k_heads, axis=-1, keepdims=True) + 1e-06)
    ).astype(jnp.bfloat16)
    q_five = q_norm.reshape(pairs_here, length, kv_local, share, HEAD_DIM)
    k_four = k_norm.reshape(pairs_here, length, kv_local, HEAD_DIM)
    v_four = values.reshape(pairs_here, length, kv_local, HEAD_DIM)
    scores = jnp.einsum("pqkgd,pskd->pkgqs", q_five, k_four, preferred_element_type=jnp.float32) * (
        score_scale / HEAD_DIM
    )
    expo = jnp.exp(scores)
    weights = (expo / jnp.sum(expo, axis=-1, keepdims=True)).astype(jnp.bfloat16)
    context = jnp.einsum(
        "pkgqs,pskd->pqkgd", weights, v_four, preferred_element_type=jnp.float32
    ).astype(jnp.bfloat16)
    context = context.reshape(pairs_here * length, kv_local * share * HEAD_DIM)
    attended = jnp.dot(context, output_weight, preferred_element_type=jnp.float32)
    head_term = jnp.mean(attended.reshape(pairs_here, length, width), axis=1)
    shares = head_term.reshape(pairs_here, tensors, feature_share).swapaxes(0, 1)
    shares = lax.all_to_all(shares, "tensor", split_axis=0, concat_axis=0, tiled=True)
    head_part = jnp.sum(shares, axis=0)
    feature_start = lax.axis_index("tensor") * feature_share
    own_features = lax.dynamic_slice_in_dim(inputs, feature_start, feature_share, 2)
    residual_mean = jnp.mean(own_features.astype(jnp.float32), axis=1)
    live = jnp.arange(pairs_here, dtype=jnp.int32) < pair_count[0]
    pooled = jnp.where(live[:, None], residual_mean + head_part, jnp.zeros_like(head_part))
    left_send = jnp.einsum(
        "pgc,pf->gcf", left_match.astype(jnp.float32), pooled, precision=lax.Precision.HIGHEST
    )
    right_send = jnp.einsum(
        "pgc,pf->gcf", right_match.astype(jnp.float32), pooled, precision=lax.Precision.HIGHEST
    )
    left_got, right_got = (
        lax.all_to_all(left_send, "group", split_axis=0, concat_axis=0, tiled=True),
        lax.all_to_all(right_send, "group", split_axis=0, concat_axis=0, tiled=True),
    )
    left_sums = owner_sums(left_owned, left_got, rows_here)
    right_sums = owner_sums(right_owned, right_got, rows_here)
    return (left_sums, right_sums)

LANES = 128
DEAD = -1
RIGHT_SHIFT = 12
DEALS = (43, 21, 34, 1, 15, 10, 61, 5, 7, 50, 11, 4)
LOADS = 8
COST = 512
WO_PARTS = 2
BF16 = jnp.bfloat16
F32 = jnp.float32


def log2(number):
    bits = number.bit_length() - 1
    assert 1 << bits == number
    return bits


def plan_sizes(groups, pairs_here):
    share = pairs_here // 2
    mean = -(-2 * share // groups)
    return (share, min(LANES // groups, (5 * mean + 1) // 2))


def column(row):
    n = row.shape[1]
    return jnp.transpose(jnp.broadcast_to(row, (n, n)))[:, :1]


def plan_body(codes, me, groups, share, cap, rows_here):
    n = codes.shape[1]
    gbits, rbits = log2(groups), log2(rows_here)
    live_total = groups * share
    live = codes >= 0
    left = jnp.where(live, codes & ((1 << RIGHT_SHIFT) - 1), 0)
    right = jnp.where(live, codes >> RIGHT_SHIFT, 0)
    left_own, right_own = left >> rbits, right >> rbits
    order = lax.broadcasted_iota(jnp.int32, (1, n), 1)
    owners = lax.broadcasted_iota(jnp.int32, (groups, n), 0)
    load_of = (left_own == owners).astype(F32) + (right_own == owners).astype(F32)
    load_of = jnp.where(live, load_of, 0.0).astype(BF16)
    live_c, left_c, right_c = column(live.astype(jnp.int32)), column(left), column(right)
    lo_c, ro_c = left_c >> rbits, right_c >> rbits
    order_c = lax.broadcasted_iota(jnp.int32, (n, 1), 0)

    def key(one, other, alive, at, deal):
        major, minor = (other, one) if deal >> 5 else (one, other)
        minor = (minor * (2 * ((deal >> 3) & 3) + 1) + (deal & 7) * major) & (groups - 1)
        return jnp.where(alive, ((major << gbits) + minor) * n, groups * groups * n) + at

    best, best_load = None, None
    for deal in DEALS:
        key_r = key(left_own, right_own, live, order, deal)
        key_c = key(lo_c, ro_c, live_c > 0, order_c, deal)
        rank = jnp.sum((key_c < key_r).astype(jnp.int32), axis=0, keepdims=True)
        to = jnp.where(rank < live_total, rank & (groups - 1), groups)
        hit = (to == owners).astype(BF16)
        load = lax.dot_general(hit, load_of, (((1,), (1,)), ((), ())), preferred_element_type=F32)
        most = jnp.max(jnp.max(load, axis=1, keepdims=True), axis=0, keepdims=True)
        if best is None:
            best, best_load = rank, most
        else:
            better = most < best_load
            best = jnp.where(better, rank, best)
            best_load = jnp.where(better, most, best_load)
    rank = best
    rank_c = column(rank)
    to_c = jnp.where(rank_c < live_total, rank_c & (groups - 1), groups)
    slot_c = rank_c >> gbits
    to = jnp.where(rank < live_total, rank & (groups - 1), groups)
    same_to = to_c == to
    earlier = jnp.logical_and(same_to, rank < rank_c)

    def count(mask):
        return jnp.sum(mask.astype(jnp.int32), axis=1, keepdims=True)

    left_pos = count(jnp.logical_and(earlier, lo_c == left_own))
    right_pos = count(jnp.logical_and(earlier, ro_c == right_own)) + count(
        jnp.logical_and(jnp.logical_and(same_to, rank < live_total), ro_c == left_own)
    )
    lane = lax.broadcasted_iota(jnp.int32, (n, LANES), 1)
    alive = rank_c < live_total

    def place(mask, at, value):
        return jnp.sum(
            jnp.where(jnp.logical_and(mask, at == lane), value, 0), axis=0, keepdims=True
        )

    left_in = jnp.logical_and(alive, left_pos < cap)
    right_in = jnp.logical_and(alive, right_pos < cap)
    local_left, local_right = left_c & (rows_here - 1), right_c & (rows_here - 1)
    send = place(
        jnp.logical_and(left_in, lo_c == me), to_c * cap + left_pos, local_left + 1
    ) + place(
        jnp.logical_and(right_in, ro_c == me), to_c * cap + right_pos, local_right + rows_here + 1
    )
    mine = jnp.logical_and(alive, to_c == me)
    fetch = place(
        jnp.logical_and(mine, left_in), slot_c * 2, lo_c * cap + left_pos
    ) + place(jnp.logical_and(mine, right_in), slot_c * 2 + 1, ro_c * cap + right_pos)
    back = to_c * share + slot_c
    left_row = place(jnp.logical_and(alive, lo_c == me), back, local_left + 1) - 1
    right_row = place(jnp.logical_and(alive, ro_c == me), back, local_right + 1) - 1
    over = jnp.broadcast_to((best_load > cap).astype(jnp.int32), (1, LANES))
    return (send, fetch, left_row, right_row, over)


def gather_cells(plan, left, right, out, sems, rows_here, cells, first, wide):
    def begin(cell, carry):
        index = plan[0, cell] - 1
        row = index & (rows_here - 1)
        for side, table in ((0, left), (1, right)):

            @pl.when(jnp.logical_and(index >= side * rows_here, index < (side + 1) * rows_here))
            def _():
                pltpu.make_async_copy(
                    table.at[row, :, pl.ds(first, wide)], out.at[cell], sems.at[cell]
                ).start()

        return carry

    def finish(cell, carry):
        @pl.when(plan[0, cell] > 0)
        def _():
            pltpu.make_async_copy(
                left.at[0, :, pl.ds(first, wide)], out.at[cell], sems.at[cell]
            ).wait()

        return carry

    lax.fori_loop(0, cells, begin, 0)
    lax.fori_loop(0, cells, finish, 0)


def plan_kernel(groups, share, cap, rows_here, wide, me, mine, others, left, right, plan_out, out, plan, sem, sems):
    rows = mine[...] + others[...]
    table = plan_body(rows, me[0], groups, share, cap, rows_here)
    for at, row in enumerate(table):
        plan_out[pl.ds(at, 1), :] = row
    copy = pltpu.make_async_copy(plan_out, plan, sem)
    copy.start()
    copy.wait()
    gather_cells(plan, left, right, out, sems, rows_here, groups * cap, 0, wide)


def gather_kernel(rows_here, cells, first, wide, plan, left, right, out, sems):
    gather_cells(plan, left, right, out, sems, rows_here, cells, first, wide)


def pick_kernel(items, after, plan, got, *refs):
    out, held, sems = refs[after:]

    def begin(item, carry):
        pltpu.make_async_copy(got.at[plan[1, item]], held.at[item], sems.at[item]).start()
        return carry

    def finish(item, carry):
        pltpu.make_async_copy(got.at[0], held.at[item], sems.at[item]).wait()
        return carry

    lax.fori_loop(0, items, begin, 0)
    lax.fori_loop(0, items, finish, 0)
    out[...] = held[...].reshape(out.shape)


def products(x_refs, gain, weights, first, ready=None):
    rows, wide = sum(x.shape[0] for x in x_refs), x_refs[0].shape[1]
    block = wide // LOADS
    widths = [w.shape[1] for w in weights]

    def one(i, carry):
        sums, square = carry
        if ready is not None:
            ready(i)
        at = pl.multiple_of(i * block, block)
        x = jnp.concatenate([x[:, pl.ds(at, block)] for x in x_refs], axis=0).astype(F32)
        normed = (x * gain[:, pl.ds(first + at, block)]).astype(BF16)
        sums = tuple(
            total + jnp.dot(normed, w[pl.ds(at, block), :], preferred_element_type=F32)
            for total, w in zip(sums, weights)
        )
        return (sums, square + jnp.sum(x * x, axis=1, keepdims=True))

    zero = (tuple(jnp.zeros((rows, n), F32) for n in widths), jnp.zeros((rows, 1), F32))
    sums, square = lax.fori_loop(0, LOADS, one, zero)
    return (jnp.concatenate(sums, axis=1), square)


def qkv_kernel(shards, first, loads, keep, extra, more, resid, after, pair_rows, *refs):
    refs = list(refs)
    x_refs = [refs.pop(0) for _ in range(shards)]
    gain = refs.pop(0)
    sources = [refs.pop(0) for _ in range(3)]
    before = [refs.pop(0) for _ in range(2)] if more else None
    extra_source = refs.pop(0) if extra is not None else None
    del refs[:after]
    sums_out, square_out = refs.pop(0), refs.pop(0)
    resid_out = refs.pop(0) if resid else None
    ready, weights = None, sources
    if keep:
        weights = [refs.pop(0) for _ in range(3)]
    extra_held = refs.pop(0) if extra is not None else None
    if loads and not keep:
        weights = [refs.pop(0) for _ in range(3)]
    if loads:
        sems = refs.pop(0)
        block = x_refs[0].shape[1] // LOADS

        def copy(which, i):
            at = i * block
            return pltpu.make_async_copy(
                sources[which].at[pl.ds(first + at, block)],
                weights[which].at[pl.ds(at, block)],
                sems.at[which, i],
            )

        for i in range(LOADS):
            for which in range(3):
                copy(which, i).start()

        def ready(i):
            for which in range(3):
                copy(which, i).wait()

    if extra is not None:
        extra_copy = pltpu.make_async_copy(
            extra_source.at[pl.ds(extra, extra_held.shape[0])], extra_held, refs.pop(0)
        )
        extra_copy.start()
    sums, square = products(x_refs, gain, weights, first, ready)
    square = jnp.broadcast_to(square, (square.shape[0], LANES))
    if more:
        sums += before[0][...]
        square += before[1][...]
    sums_out[...] = sums
    square_out[...] = square
    if resid:
        rows = x_refs[0].shape[0]
        pairs = rows // pair_rows
        pair = lax.broadcasted_iota(jnp.int32, (pairs, rows), 1) // pair_rows
        mine = (pair == lax.broadcasted_iota(jnp.int32, (pairs, rows), 0)).astype(BF16)
        resid_out[...] = jnp.dot(mine, x_refs[0][...], preferred_element_type=F32)
    if extra is not None:
        extra_copy.wait()


def tail_kernel(
    shards, groups, parts, width, length, pair_rows, first, t_ref, x_ref, gain, wq, wk, wv, *refs
):
    wos, refs = refs[:WO_PARTS], refs[WO_PARTS:]
    accs, sqs, resids = refs[:groups], refs[groups : 2 * groups], refs[2 * groups : 2 * groups + parts]
    outs, (ctx, out) = refs[2 * groups + parts : -2], refs[-2:]
    pairs, features = out.shape[1:]
    heads, kv_heads = wq.shape[1] // HEAD_DIM, wk.shape[1] // HEAD_DIM
    share = heads // kv_heads
    sums, square = products([x_ref], gain, (wq, wk, wv), first)
    acc = jnp.concatenate([a[...] for a in accs[:-1]] + [accs[-1][...] + sums], axis=0)
    sq = jnp.concatenate([s[:, :1] for s in sqs[:-1]] + [sqs[-1][:, :1] + square], axis=0)
    tokens = acc.shape[0]
    acc = acc * lax.rsqrt(sq * (1.0 / width) + 1e-05)
    rows = tokens // shards
    row = lax.broadcasted_iota(jnp.int32, (share * tokens, tokens), 0)
    col = lax.broadcasted_iota(jnp.int32, (share * tokens, tokens), 1)
    same = ((row & (rows - 1)) >> log2(pair_rows)) == ((col & (rows - 1)) >> log2(pair_rows))
    pair = lax.broadcasted_iota(jnp.int32, (pairs, tokens), 0)
    token = lax.broadcasted_iota(jnp.int32, (pairs, tokens), 1)
    member = ((token & (rows - 1)) >> log2(pair_rows)) == pair
    nq, nk = heads * HEAD_DIM, kv_heads * HEAD_DIM

    def unit(part):
        return (part * lax.rsqrt(jnp.mean(part * part, axis=1, keepdims=True) + 1e-06)).astype(
            BF16
        )

    def head(start):
        return acc[:, start : start + HEAD_DIM]

    for kv in range(kv_heads):
        k = unit(head(nq + kv * HEAD_DIM))
        v = head(nq + nk + kv * HEAD_DIM).astype(BF16)
        q = jnp.concatenate(
            [unit(head((kv * share + i) * HEAD_DIM)) for i in range(share)], axis=0
        )
        scores = lax.dot_general(
            q, k, (((1,), (1,)), ((), ())), preferred_element_type=F32
        ) * (score_scale / HEAD_DIM)
        expo = jnp.where(same, jnp.exp(scores), 0.0)
        weights = expo / jnp.sum(expo, axis=1, keepdims=True)
        spread = []
        for i in range(share):
            mean = jnp.sum(weights[i * tokens : (i + 1) * tokens], axis=0, keepdims=True)
            spread.append(jnp.where(member, mean * (1.0 / length), 0.0))
        spread = jnp.concatenate(spread, axis=0)
        high = spread.astype(BF16)
        low = (spread - high.astype(F32)).astype(BF16)
        context = jnp.dot(
            jnp.concatenate([high, low], axis=0), v, preferred_element_type=F32
        )
        context = context[: share * pairs] + context[share * pairs :]
        for i in range(share):
            one_head = context[i * pairs : (i + 1) * pairs]
            high = one_head.astype(BF16)
            low = (one_head - high.astype(F32)).astype(BF16)
            at = (kv * share + i) * HEAD_DIM
            ctx[:, at : at + HEAD_DIM] = jnp.concatenate([high, low], axis=0)

    block = min(512, features)
    per = features // block
    done = 0
    for resid in resids:

        def one(i, carry):
            here = pl.multiple_of(i * block, block)
            i = i + done // block
            at = pl.multiple_of(i * block, block)
            deep = wos[0].shape[0]
            both = sum(
                jnp.dot(
                    ctx[:, j * deep : (j + 1) * deep],
                    wo[:, pl.ds(at, block)],
                    preferred_element_type=F32,
                )
                for j, wo in enumerate(wos)
            )
            both = both[:pairs] + both[pairs:] + resid[:, pl.ds(here, block)] * (1.0 / length)
            inside = pl.multiple_of((i % per) * block, block)
            out[pl.ds((i // per) ^ t_ref[0], 1), :, pl.ds(inside, block)] = both[None]
            return carry

        lax.fori_loop(0, resid.shape[1] // block, one, 0)
        done += resid.shape[1]
    for i, piece in enumerate(outs):
        piece[...] = out[i].astype(piece.dtype)


def final_kernel(plan, pooled, left, right, held, sems):
    rows, n = left.shape[0], pooled.shape[0]
    at = lax.broadcasted_iota(jnp.int32, (rows, n), 0)
    copies = []
    for side, out in enumerate((left, right)):
        hit = (plan[pl.ds(2 + side, 1), :][:, :n] == at).astype(BF16)
        held[side] = jnp.dot(hit, pooled[...], preferred_element_type=F32)
        copies.append(pltpu.make_async_copy(held.at[side], out, sems.at[side]))
        copies[-1].start()
    for copy in copies:
        copy.wait()


ANY = pl.BlockSpec(memory_space=pl.ANY)
IN_VMEM = pl.BlockSpec(memory_space=pltpu.VMEM)
IN_SMEM = pl.BlockSpec(memory_space=pltpu.SMEM)
LIMIT = pltpu.CompilerParams(vmem_limit_bytes=6 * 1024 * 1024)
WIDE_LIMIT = pltpu.CompilerParams(vmem_limit_bytes=24 * 1024 * 1024)


def shape(dims, kind):
    return jax.ShapeDtypeStruct(dims, kind)


def held_in_vmem(array):
    return pltpu.with_memory_space_constraint(array, pltpu.VMEM)


def qkv(xs, first, gain, weights, loads, keep, before, resid, pair_rows, extra=None, after=()):
    rows, wide = sum(x.shape[0] for x in xs), xs[0].shape[1]
    total = sum(w.shape[1] for w in weights)
    args = [*xs, gain, *weights] + (before or [])
    in_specs = [IN_VMEM] * (len(xs) + 1) + [ANY if loads else IN_VMEM] * 3
    in_specs += [IN_VMEM] * len(before or [])
    out_shape = [shape((rows, total), F32), shape((rows, LANES), F32)]
    scratch = []
    if resid:
        out_shape.append(shape((xs[0].shape[0] // pair_rows, wide), F32))
    if loads:
        halves = [pltpu.VMEM((wide, w.shape[1]), w.dtype) for w in weights]
        if keep:
            out_shape += halves
        else:
            scratch += halves
        scratch.append(pltpu.SemaphoreType.DMA((3, LOADS)))
    if extra is not None:
        array, part, at = extra
        args.append(array)
        in_specs.append(ANY)
        out_shape.append(pltpu.VMEM((part, array.shape[1]), array.dtype))
        scratch.append(pltpu.SemaphoreType.DMA(()))
    args += after
    in_specs += [ANY] * len(after)
    out = pl.pallas_call(
        functools.partial(
            qkv_kernel,
            len(xs),
            first,
            loads,
            keep,
            None if extra is None else extra[2],
            before is not None,
            resid,
            len(after),
            pair_rows,
        ),
        in_specs=in_specs,
        out_specs=[IN_VMEM] * len(out_shape),
        out_shape=out_shape,
        scratch_shapes=scratch,
        compiler_params=LIMIT if keep or not loads else WIDE_LIMIT,
        cost_estimate=pl.CostEstimate(
            flops=COST * wide * total, bytes_accessed=2 * rows * wide, transcendentals=0
        ),
    )(*args)
    out = list(out)
    result = {"sums": [out.pop(0), out.pop(0)]}
    if resid:
        result["resid"] = out.pop(0)
    if keep:
        result["weights"] = [held_in_vmem(out.pop(0)) for _ in range(3)]
    if extra is not None:
        result["extra"] = held_in_vmem(out.pop(0))
    return result


def on_device(
    left_table,
    right_table,
    left_owner,
    left_row,
    right_owner,
    right_row,
    pair_count,
    norm_gain,
    query_weight,
    key_weight,
    value_weight,
    output_weight,
):
    groups = lax.axis_size("group")
    tensors = lax.axis_size("tensor")
    group, tensor = lax.axis_index("group"), lax.axis_index("tensor")
    pairs_here = left_owner.shape[0]
    rows_here, toks, width = left_table.shape
    share, cap = plan_sizes(groups, pairs_here)
    cells, items = groups * cap, 2 * share
    rows = items * toks
    pair_rows = 2 * toks
    length = pair_rows * tensors
    features = width // tensors
    n = groups * pairs_here

    code = (left_owner[:, 0] * rows_here + left_row) | (
        (right_owner[:, 0] * rows_here + right_row) << RIGHT_SHIFT
    )
    code = jnp.where(jnp.arange(pairs_here, dtype=jnp.int32) < pair_count[0], code, DEAD)
    at = jnp.arange(n, dtype=jnp.int32) // pairs_here
    code = jnp.where(at == group, jnp.tile(code, groups), 0)[None, :]
    hop = 1
    while hop < groups:
        codes = [code, lax.ppermute(code, "group", [(i, i ^ hop) for i in range(groups)])]
        code, hop = codes[0] + codes[1], 2 * hop

    head = width * 5 // 8
    parts = ((0, head), (head, width - head))
    me = jnp.reshape(group, (1,)).astype(jnp.int32)
    plan, cell_rows = pl.pallas_call(
        functools.partial(plan_kernel, groups, share, cap, rows_here, parts[0][1]),
        in_specs=[IN_SMEM, IN_VMEM, IN_VMEM, ANY, ANY],
        out_specs=[IN_VMEM, IN_VMEM],
        out_shape=[shape((8, LANES), jnp.int32), shape((cells, toks, parts[0][1]), BF16)],
        scratch_shapes=[
            pltpu.SMEM((8, LANES), jnp.int32),
            pltpu.SemaphoreType.DMA(()),
            pltpu.SemaphoreType.DMA((cells,)),
        ],
        compiler_params=LIMIT,
    )(me, *codes, left_table, right_table)
    sends = [cell_rows]
    for first, wide in parts[1:]:
        sends.append(
            pl.pallas_call(
                functools.partial(gather_kernel, rows_here, cells, first, wide),
                in_specs=[IN_SMEM, ANY, ANY],
                out_specs=IN_VMEM,
                out_shape=shape((cells, toks, wide), BF16),
                scratch_shapes=[pltpu.SemaphoreType.DMA((cells,))],
                compiler_params=LIMIT,
            )(plan, left_table, right_table)
        )
    gain = norm_gain[None, :]
    weights = (query_weight, key_weight, value_weight)
    ring = [(i, (i + 1) % tensors) for i in range(tensors)]

    def exchange(send):
        return lax.all_to_all(send, "group", split_axis=0, concat_axis=0, tiled=True)

    def pick(got, after):
        wide = got.shape[2]
        return pl.pallas_call(
            functools.partial(pick_kernel, items, len(after)),
            in_specs=[IN_SMEM, ANY] + [ANY] * len(after),
            out_specs=IN_VMEM,
            out_shape=shape((rows, wide), BF16),
            scratch_shapes=[
                pltpu.VMEM((items, toks, wide), BF16),
                pltpu.SemaphoreType.DMA((items,)),
            ],
            compiler_params=LIMIT,
        )(plan, got, *after)

    def pass_on(x):
        return lax.ppermute(x, "tensor", ring)

    one, two = [[pick(exchange(sends[0]), [])], []]
    first = qkv(one, parts[0][0], gain, weights, True, False, None, True, pair_rows)
    one.append(pass_on(one[0]))
    two.append(pick(exchange(sends[1]), [first["sums"][1], one[1]]))
    for _ in range(2, tensors):
        one.append(pass_on(one[-1]))
    for _ in range(1, tensors):
        two.append(pass_on(two[-1]))
    shards = [(0, 1), (1, 3)] + [(i, i + 1) for i in range(3, tensors)]
    deep = output_weight.shape[0] // WO_PARTS
    sums, wos, held_one, held_two = [first["sums"]], [], None, None
    for low, high in shards[1:]:
        out = qkv(
            one[low:high],
            parts[0][0],
            gain,
            held_one or weights,
            held_one is None,
            held_one is None,
            None,
            False,
            pair_rows,
            (output_weight, deep, 0) if low == 3 else None,
            [two[0]] if held_one is None else [],
        )
        held_one = held_one or out["weights"]
        sums.append(out["sums"])
        if "extra" in out:
            wos.append(out["extra"])
    resids = [first["resid"]]
    for at, (low, high) in enumerate(shards[:-1]):
        out = qkv(
            two[low:high],
            parts[1][0],
            gain,
            held_two or weights,
            held_two is None,
            held_two is None,
            sums[at],
            low == 0,
            pair_rows,
            (output_weight, deep, deep) if low == 1 else None,
        )
        held_two = held_two or out["weights"]
        sums[at] = out["sums"]
        if low == 0:
            resids.append(out["resid"])
        if "extra" in out:
            wos.append(out["extra"])
    held, held_weights = two, [held_two]
    accs, sqs = [s[0] for s in sums], [s[1] for s in sums]

    args = [held[-1], gain, *held_weights[-1], *wos, *accs, *sqs, *resids]
    partial_sums = pl.pallas_call(
        functools.partial(
            tail_kernel, tensors, len(shards), len(parts), width, length, pair_rows, parts[-1][0]
        ),
        in_specs=[IN_SMEM] + [IN_VMEM] * len(args),
        out_specs=[IN_VMEM] * tensors,
        out_shape=[shape((share, features), F32)]
        + [shape((share, features), BF16)] * (tensors - 1),
        scratch_shapes=[
            pltpu.VMEM((2 * share, output_weight.shape[0]), BF16),
            pltpu.VMEM((tensors, share, features), F32),
        ],
        compiler_params=LIMIT,
        cost_estimate=pl.CostEstimate(
            flops=32 * share * width * output_weight.shape[0],
            bytes_accessed=2 * rows * width,
            transcendentals=0,
        ),
    )(jnp.reshape(tensor, (1,)).astype(jnp.int32), *args)
    pooled = partial_sums[0]
    for step in range(1, tensors):
        swap = [(i, i ^ step) for i in range(tensors)]
        pooled = pooled + lax.ppermute(partial_sums[step], "tensor", swap).astype(F32)
    everyone = lax.all_gather(pooled.astype(BF16), "group", tiled=True)

    def fast():
        return tuple(
            pl.pallas_call(
                final_kernel,
                in_specs=[IN_VMEM, IN_VMEM],
                out_specs=[ANY, ANY],
                out_shape=[pltpu.HBM((rows_here, features), F32)] * 2,
                scratch_shapes=[
                    pltpu.VMEM((2, rows_here, features), F32),
                    pltpu.SemaphoreType.DMA((2,)),
                ],
                compiler_params=LIMIT,
            )(plan, everyone)
        )

    def general():
        return general_program(
            left_table,
            right_table,
            left_owner,
            left_row,
            right_owner,
            right_row,
            pair_count,
            norm_gain,
            query_weight,
            key_weight,
            value_weight,
            output_weight,
        )

    return lax.cond(plan[4, 0] > 0, general, fast)


def solution(mesh):
    return jax.shard_map(
        on_device,
        mesh=mesh,
        in_specs=(
            P("group", "tensor", None),
            P("group", "tensor", None),
            P("group", None),
            P("group"),
            P("group", None),
            P("group"),
            P("group"),
            P(),
            P(None, "tensor"),
            P(None, "tensor"),
            P(None, "tensor"),
            P("tensor", None),
        ),
        out_specs=(P("group", "tensor"), P("group", "tensor")),
        check_vma=False,
    )
```

```python
import functools

import jax
import jax.numpy as jnp
from jax import lax
from jax.experimental import pallas as pl
from jax.experimental.pallas import tpu as pltpu
from jax.sharding import PartitionSpec as P

HEAD_DIM = 128


score_scale = 4.0


def slot_plan(owner, groups, capacity):
    count = owner.shape[0]
    order = jnp.arange(count, dtype=jnp.int32)
    same_owner = owner[:, None] == owner[None, :]
    earlier = order[None, :] < order[:, None]
    rank = jnp.sum(jnp.logical_and(same_owner, earlier), axis=1)
    owner_hit = owner[:, None, None] == jnp.arange(groups, dtype=jnp.int32)[None, :, None]
    rank_hit = rank[:, None, None] == jnp.arange(capacity, dtype=jnp.int32)[None, None, :]
    return (rank, jnp.logical_and(owner_hit, rank_hit))


def request_ids(slot_match, row_index):
    return jnp.sum(jnp.where(slot_match, row_index[:, None, None], 0), axis=0)


def owner_sums(row_ids, arrived, rows_here):
    onehot = (row_ids[:, :, None] == jnp.arange(rows_here, dtype=jnp.int32)[None, None, :]).astype(
        jnp.float32
    )
    return jnp.einsum("gcr,gcf->rf", onehot, arrived, precision=lax.Precision.HIGHEST)


def general_program(
    left_table,
    right_table,
    left_owner,
    left_row,
    right_owner,
    right_row,
    pair_count,
    norm_gain,
    query_weight,
    key_weight,
    value_weight,
    output_weight,
):
    groups = lax.axis_size("group")
    tensors = lax.axis_size("tensor")
    pairs_here = left_owner.shape[0]
    capacity = 2 * pairs_here // groups
    rows_here = left_table.shape[0]
    width = left_table.shape[2]
    feature_share = width // tensors
    left_group = left_owner[:, 0]
    right_group = right_owner[:, 0]
    left_rank, left_match = slot_plan(left_group, groups, capacity)
    right_rank, right_match = slot_plan(right_group, groups, capacity)
    left_request = request_ids(left_match, left_row)
    right_request = request_ids(right_match, right_row)
    left_spread = jnp.broadcast_to(left_request[:, None, :], (groups, tensors, capacity)).reshape(
        groups * tensors, capacity
    )
    right_spread = jnp.broadcast_to(right_request[:, None, :], (groups, tensors, capacity)).reshape(
        groups * tensors, capacity
    )
    left_wanted, right_wanted = (
        lax.all_to_all(left_spread, ("group", "tensor"), split_axis=0, concat_axis=0, tiled=True),
        lax.all_to_all(right_spread, ("group", "tensor"), split_axis=0, concat_axis=0, tiled=True),
    )
    left_back, right_back = (
        lax.all_to_all(
            left_table[left_wanted], ("group", "tensor"), split_axis=0, concat_axis=0, tiled=True
        ),
        lax.all_to_all(
            right_table[right_wanted], ("group", "tensor"), split_axis=0, concat_axis=0, tiled=True
        ),
    )
    left_back = left_back.reshape(groups, tensors, capacity, left_table.shape[1], width)
    right_back = right_back.reshape(groups, tensors, capacity, right_table.shape[1], width)
    left_tokens = left_back[left_group, :, left_rank].reshape(
        pairs_here, tensors * left_table.shape[1], width
    )
    right_tokens = right_back[right_group, :, right_rank].reshape(
        pairs_here, tensors * right_table.shape[1], width
    )
    left_owned = left_wanted.reshape(groups, tensors, capacity)[:, 0]
    right_owned = right_wanted.reshape(groups, tensors, capacity)[:, 0]
    inputs = jnp.concatenate([left_tokens, right_tokens], axis=1)
    length = inputs.shape[1]
    flat = inputs.reshape(pairs_here * length, width)
    wide = flat.astype(jnp.float32)
    scale = lax.rsqrt(jnp.mean(wide * wide, axis=-1, keepdims=True) + 1e-05)
    normed = (wide * scale * norm_gain[None, :]).astype(jnp.bfloat16)
    q_raw = jnp.dot(normed, query_weight, preferred_element_type=jnp.float32)
    k_raw = jnp.dot(normed, key_weight, preferred_element_type=jnp.float32)
    values = jnp.dot(normed, value_weight, preferred_element_type=jnp.float32).astype(jnp.bfloat16)
    kv_local = key_weight.shape[1] // HEAD_DIM
    share = query_weight.shape[1] // HEAD_DIM // kv_local
    q_heads = q_raw.reshape(pairs_here * length, kv_local * share, HEAD_DIM)
    k_heads = k_raw.reshape(pairs_here * length, kv_local, HEAD_DIM)
    q_norm = (
        q_heads * lax.rsqrt(jnp.mean(q_heads * q_heads, axis=-1, keepdims=True) + 1e-06)
    ).astype(jnp.bfloat16)
    k_norm = (
        k_heads * lax.rsqrt(jnp.mean(k_heads * k_heads, axis=-1, keepdims=True) + 1e-06)
    ).astype(jnp.bfloat16)
    q_five = q_norm.reshape(pairs_here, length, kv_local, share, HEAD_DIM)
    k_four = k_norm.reshape(pairs_here, length, kv_local, HEAD_DIM)
    v_four = values.reshape(pairs_here, length, kv_local, HEAD_DIM)
    scores = jnp.einsum("pqkgd,pskd->pkgqs", q_five, k_four, preferred_element_type=jnp.float32) * (
        score_scale / HEAD_DIM
    )
    expo = jnp.exp(scores)
    weights = (expo / jnp.sum(expo, axis=-1, keepdims=True)).astype(jnp.bfloat16)
    context = jnp.einsum(
        "pkgqs,pskd->pqkgd", weights, v_four, preferred_element_type=jnp.float32
    ).astype(jnp.bfloat16)
    context = context.reshape(pairs_here * length, kv_local * share * HEAD_DIM)
    attended = jnp.dot(context, output_weight, preferred_element_type=jnp.float32)
    head_term = jnp.mean(attended.reshape(pairs_here, length, width), axis=1)
    shares = head_term.reshape(pairs_here, tensors, feature_share).swapaxes(0, 1)
    shares = lax.all_to_all(shares, "tensor", split_axis=0, concat_axis=0, tiled=True)
    head_part = jnp.sum(shares, axis=0)
    feature_start = lax.axis_index("tensor") * feature_share
    own_features = lax.dynamic_slice_in_dim(inputs, feature_start, feature_share, 2)
    residual_mean = jnp.mean(own_features.astype(jnp.float32), axis=1)
    live = jnp.arange(pairs_here, dtype=jnp.int32) < pair_count[0]
    pooled = jnp.where(live[:, None], residual_mean + head_part, jnp.zeros_like(head_part))
    left_send = jnp.einsum(
        "pgc,pf->gcf", left_match.astype(jnp.float32), pooled, precision=lax.Precision.HIGHEST
    )
    right_send = jnp.einsum(
        "pgc,pf->gcf", right_match.astype(jnp.float32), pooled, precision=lax.Precision.HIGHEST
    )
    left_got, right_got = (
        lax.all_to_all(left_send, "group", split_axis=0, concat_axis=0, tiled=True),
        lax.all_to_all(right_send, "group", split_axis=0, concat_axis=0, tiled=True),
    )
    left_sums = owner_sums(left_owned, left_got, rows_here)
    right_sums = owner_sums(right_owned, right_got, rows_here)
    return (left_sums, right_sums)

LANES = 128
DEAD = -1
RIGHT_SHIFT = 12
DEALS = (43, 21, 34, 1, 15, 10, 61, 5, 7, 50, 11, 4)
LOADS = 8
BLOCK = 512
COST = 512
WO_PARTS = 2
BF16 = jnp.bfloat16
F32 = jnp.float32


def log2(number):
    bits = number.bit_length() - 1
    assert 1 << bits == number
    return bits


def plan_sizes(groups, pairs_here):
    share = pairs_here // 2
    mean = -(-2 * share // groups)
    return (share, min(LANES // groups, (5 * mean + 1) // 2))


def column(row):
    n = row.shape[1]
    return jnp.transpose(jnp.broadcast_to(row, (n, n)))[:, :1]


def split3(wide):
    high = wide.astype(BF16)
    rest = wide - high.astype(F32)
    mid = rest.astype(BF16)
    low = (rest - mid.astype(F32)).astype(BF16)
    return (high, mid, low)


def plan_body(codes, me, groups, share, cap, rows_here):
    n = codes.shape[1]
    gbits, rbits = log2(groups), log2(rows_here)
    live_total = groups * share
    live = codes >= 0
    left = jnp.where(live, codes & ((1 << RIGHT_SHIFT) - 1), 0)
    right = jnp.where(live, codes >> RIGHT_SHIFT, 0)
    left_own, right_own = left >> rbits, right >> rbits
    order = lax.broadcasted_iota(jnp.int32, (1, n), 1)
    owners = lax.broadcasted_iota(jnp.int32, (groups, n), 0)
    load_of = (left_own == owners).astype(F32) + (right_own == owners).astype(F32)
    load_of = jnp.where(live, load_of, 0.0).astype(BF16)
    live_c, left_c, right_c = column(live.astype(jnp.int32)), column(left), column(right)
    lo_c, ro_c = left_c >> rbits, right_c >> rbits
    order_c = lax.broadcasted_iota(jnp.int32, (n, 1), 0)

    def key(one, other, alive, at, deal):
        major, minor = (other, one) if deal >> 5 else (one, other)
        minor = (minor * (2 * ((deal >> 3) & 3) + 1) + (deal & 7) * major) & (groups - 1)
        return jnp.where(alive, ((major << gbits) + minor) * n, groups * groups * n) + at

    best, best_load = None, None
    for deal in DEALS:
        key_r = key(left_own, right_own, live, order, deal)
        key_c = key(lo_c, ro_c, live_c > 0, order_c, deal)
        rank = jnp.sum((key_c < key_r).astype(jnp.int32), axis=0, keepdims=True)
        to = jnp.where(rank < live_total, rank & (groups - 1), groups)
        hit = (to == owners).astype(BF16)
        load = lax.dot_general(hit, load_of, (((1,), (1,)), ((), ())), preferred_element_type=F32)
        most = jnp.max(jnp.max(load, axis=1, keepdims=True), axis=0, keepdims=True)
        if best is None:
            best, best_load = rank, most
        else:
            better = most < best_load
            best = jnp.where(better, rank, best)
            best_load = jnp.where(better, most, best_load)
    rank = best
    rank_c = column(rank)
    to_c = jnp.where(rank_c < live_total, rank_c & (groups - 1), groups)
    slot_c = rank_c >> gbits
    to = jnp.where(rank < live_total, rank & (groups - 1), groups)
    same_to = to_c == to
    earlier = jnp.logical_and(same_to, rank < rank_c)

    def count(mask):
        return jnp.sum(mask.astype(jnp.int32), axis=1, keepdims=True)

    left_pos = count(jnp.logical_and(earlier, lo_c == left_own))
    right_pos = count(jnp.logical_and(earlier, ro_c == right_own)) + count(
        jnp.logical_and(jnp.logical_and(same_to, rank < live_total), ro_c == left_own)
    )
    lane = lax.broadcasted_iota(jnp.int32, (n, LANES), 1)
    alive = rank_c < live_total

    def place(mask, at, value):
        return jnp.sum(
            jnp.where(jnp.logical_and(mask, at == lane), value, 0), axis=0, keepdims=True
        )

    left_in = jnp.logical_and(alive, left_pos < cap)
    right_in = jnp.logical_and(alive, right_pos < cap)
    local_left, local_right = left_c & (rows_here - 1), right_c & (rows_here - 1)
    send = place(
        jnp.logical_and(left_in, lo_c == me), to_c * cap + left_pos, local_left + 1
    ) + place(
        jnp.logical_and(right_in, ro_c == me), to_c * cap + right_pos, local_right + rows_here + 1
    )
    mine = jnp.logical_and(alive, to_c == me)
    fetch = place(
        jnp.logical_and(mine, left_in), slot_c * 2, lo_c * cap + left_pos
    ) + place(jnp.logical_and(mine, right_in), slot_c * 2 + 1, ro_c * cap + right_pos)
    back = to_c * share + slot_c
    left_row = place(jnp.logical_and(alive, lo_c == me), back, local_left + 1) - 1
    right_row = place(jnp.logical_and(alive, ro_c == me), back, local_right + 1) - 1
    over = jnp.broadcast_to((best_load > cap).astype(jnp.int32), (1, LANES))
    return (send, fetch, left_row, right_row, over)


def gather_cells(plan, left, right, out, sems, rows_here, cells, first, wide):
    def begin(cell, carry):
        index = plan[0, cell] - 1
        row = index & (rows_here - 1)
        for side, table in ((0, left), (1, right)):

            @pl.when(jnp.logical_and(index >= side * rows_here, index < (side + 1) * rows_here))
            def _():
                pltpu.make_async_copy(
                    table.at[row, :, pl.ds(first, wide)], out.at[cell], sems.at[cell]
                ).start()

        return carry

    def finish(cell, carry):
        @pl.when(plan[0, cell] > 0)
        def _():
            pltpu.make_async_copy(
                left.at[0, :, pl.ds(first, wide)], out.at[cell], sems.at[cell]
            ).wait()

        return carry

    lax.fori_loop(0, cells, begin, 0)
    lax.fori_loop(0, cells, finish, 0)


def plan_kernel(groups, share, cap, rows_here, wide, me, mine, others, left, right, plan_out, out, plan, sem, sems):
    rows = mine[...] + others[...]
    table = plan_body(rows, me[0], groups, share, cap, rows_here)
    for at, row in enumerate(table):
        plan_out[pl.ds(at, 1), :] = row
    copy = pltpu.make_async_copy(plan_out, plan, sem)
    copy.start()
    copy.wait()
    gather_cells(plan, left, right, out, sems, rows_here, groups * cap, 0, wide)


def gather_kernel(rows_here, cells, first, wide, plan, left, right, out, sems):
    gather_cells(plan, left, right, out, sems, rows_here, cells, first, wide)


def pick_kernel(items, after, plan, got, *refs):
    out, held, sems = refs[after:]

    def begin(item, carry):
        pltpu.make_async_copy(got.at[plan[1, item]], held.at[item], sems.at[item]).start()
        return carry

    def finish(item, carry):
        pltpu.make_async_copy(got.at[0], held.at[item], sems.at[item]).wait()
        return carry

    lax.fori_loop(0, items, begin, 0)
    lax.fori_loop(0, items, finish, 0)
    out[...] = held[...].reshape(out.shape)


def products(x_refs, gain, weights, first, ready=None):
    rows, wide = sum(x.shape[0] for x in x_refs), x_refs[0].shape[1]
    block = BLOCK
    widths = [w.shape[1] for w in weights]

    def one(i, carry):
        sums, square = carry
        if ready is not None:
            ready(i)
        at = pl.multiple_of(i * block, block)
        x = jnp.concatenate([x[:, pl.ds(at, block)] for x in x_refs], axis=0).astype(F32)
        normed = (x * gain[:, pl.ds(first + at, block)]).astype(BF16)
        sums = tuple(
            total + jnp.dot(normed, w[pl.ds(at, block), :], preferred_element_type=F32)
            for total, w in zip(sums, weights)
        )
        return (sums, square + jnp.sum(x * x, axis=1, keepdims=True))

    zero = (tuple(jnp.zeros((rows, n), F32) for n in widths), jnp.zeros((rows, 1), F32))
    sums, square = lax.fori_loop(0, wide // block, one, zero)
    return (jnp.concatenate(sums, axis=1), square)


def qkv_kernel(shards, first, loads, keep, extra, more, resid, after, pair_rows, *refs):
    refs = list(refs)
    x_refs = [refs.pop(0) for _ in range(shards)]
    gain = refs.pop(0)
    sources = [refs.pop(0) for _ in range(3)]
    before = [refs.pop(0) for _ in range(2)] if more else None
    extra_source = refs.pop(0) if extra is not None else None
    del refs[:after]
    sums_out, square_out = refs.pop(0), refs.pop(0)
    resid_out = refs.pop(0) if resid else None
    ready, weights = None, sources
    if keep:
        weights = [refs.pop(0) for _ in range(3)]
    extra_held = refs.pop(0) if extra is not None else None
    if loads and not keep:
        weights = [refs.pop(0) for _ in range(3)]
    if loads:
        sems = refs.pop(0)
        block = BLOCK

        def copy(which, i):
            at = i * block
            return pltpu.make_async_copy(
                sources[which].at[pl.ds(first + at, block)],
                weights[which].at[pl.ds(at, block)],
                sems.at[which, i],
            )

        for i in range(x_refs[0].shape[1] // block):
            for which in range(3):
                copy(which, i).start()

        def ready(i):
            for which in range(3):
                copy(which, i).wait()

    if extra is not None:
        extra_copy = pltpu.make_async_copy(
            extra_source.at[pl.ds(extra, extra_held.shape[0])], extra_held, refs.pop(0)
        )
        extra_copy.start()
    sums, square = products(x_refs, gain, weights, first, ready)
    square = jnp.broadcast_to(square, (square.shape[0], LANES))
    if more:
        sums += before[0][...]
        square += before[1][...]
    sums_out[...] = sums
    square_out[...] = square
    if resid:
        rows = x_refs[0].shape[0]
        pairs = rows // pair_rows
        pair = lax.broadcasted_iota(jnp.int32, (pairs, rows), 1) // pair_rows
        mine = (pair == lax.broadcasted_iota(jnp.int32, (pairs, rows), 0)).astype(BF16)
        resid_out[...] = jnp.dot(mine, x_refs[0][...], preferred_element_type=F32)
    if extra is not None:
        extra_copy.wait()


def tail_kernel(
    shards, groups, parts, width, length, pair_rows, first, t_ref, x_ref, gain, wq, wk, wv, *refs
):
    wos, refs = refs[:WO_PARTS], refs[WO_PARTS:]
    accs, sqs, resids = refs[:groups], refs[groups : 2 * groups], refs[2 * groups : 2 * groups + parts]
    outs, (ctx, out, wo_tail, sems) = refs[2 * groups + parts : -4], refs[-4:]
    deep = wo_tail.shape[0]
    copies = [
        pltpu.make_async_copy(
            wos[1].at[pl.ds(deep + i * (deep // LOADS), deep // LOADS)],
            wo_tail.at[pl.ds(i * (deep // LOADS), deep // LOADS)],
            sems.at[i],
        )
        for i in range(LOADS)
    ]
    for copy in copies:
        copy.start()
    wos = [wos[0], wo_tail]
    pairs, features = out.shape[1:]
    heads, kv_heads = wq.shape[1] // HEAD_DIM, wk.shape[1] // HEAD_DIM
    share = heads // kv_heads
    sums, square = products([x_ref], gain, (wq, wk, wv), first)
    acc = jnp.concatenate([a[...] for a in accs[:-1]] + [accs[-1][...] + sums], axis=0)
    sq = jnp.concatenate([s[:, :1] for s in sqs[:-1]] + [sqs[-1][:, :1] + square], axis=0)
    tokens = acc.shape[0]
    acc = acc * lax.rsqrt(sq * (1.0 / width) + 1e-05)
    rows = tokens // shards
    row = lax.broadcasted_iota(jnp.int32, (share * tokens, tokens), 0)
    col = lax.broadcasted_iota(jnp.int32, (share * tokens, tokens), 1)
    same = ((row & (rows - 1)) >> log2(pair_rows)) == ((col & (rows - 1)) >> log2(pair_rows))
    pair = lax.broadcasted_iota(jnp.int32, (pairs, tokens), 0)
    token = lax.broadcasted_iota(jnp.int32, (pairs, tokens), 1)
    member = ((token & (rows - 1)) >> log2(pair_rows)) == pair
    nq, nk = heads * HEAD_DIM, kv_heads * HEAD_DIM

    def unit(part):
        return (part * lax.rsqrt(jnp.mean(part * part, axis=1, keepdims=True) + 1e-06)).astype(
            BF16
        )

    def head(start):
        return acc[:, start : start + HEAD_DIM]

    for kv in range(kv_heads):
        k = unit(head(nq + kv * HEAD_DIM))
        v = head(nq + nk + kv * HEAD_DIM).astype(BF16)
        q = jnp.concatenate(
            [unit(head((kv * share + i) * HEAD_DIM)) for i in range(share)], axis=0
        )
        scores = lax.dot_general(
            q, k, (((1,), (1,)), ((), ())), preferred_element_type=F32
        ) * (score_scale / HEAD_DIM)
        expo = jnp.where(same, jnp.exp(scores), 0.0)
        weights = expo / jnp.sum(expo, axis=1, keepdims=True)
        spread = []
        for i in range(share):
            mean = jnp.sum(weights[i * tokens : (i + 1) * tokens], axis=0, keepdims=True)
            spread.append(jnp.where(member, mean * (1.0 / length), 0.0))
        spread = jnp.concatenate(spread, axis=0)
        high = spread.astype(BF16)
        low = (spread - high.astype(F32)).astype(BF16)
        context = jnp.dot(
            jnp.concatenate([high, low], axis=0), v, preferred_element_type=F32
        )
        context = context[: share * pairs] + context[share * pairs :]
        for i in range(share):
            one_head = context[i * pairs : (i + 1) * pairs]
            high = one_head.astype(BF16)
            low = (one_head - high.astype(F32)).astype(BF16)
            at = (kv * share + i) * HEAD_DIM
            ctx[:, at : at + HEAD_DIM] = jnp.concatenate([high, low], axis=0)

    for copy in copies:
        copy.wait()
    block = min(512, features)
    per = features // block
    done = 0
    for resid in resids:

        def one(i, carry):
            here = pl.multiple_of(i * block, block)
            i = i + done // block
            at = pl.multiple_of(i * block, block)
            both = sum(
                jnp.dot(
                    ctx[:, j * deep : (j + 1) * deep],
                    wo[:, pl.ds(at, block)],
                    preferred_element_type=F32,
                )
                for j, wo in enumerate(wos)
            )
            both = both[:pairs] + both[pairs:] + resid[:, pl.ds(here, block)] * (1.0 / length)
            inside = pl.multiple_of((i % per) * block, block)
            out[pl.ds((i // per) ^ t_ref[0], 1), :, pl.ds(inside, block)] = both[None]
            return carry

        lax.fori_loop(0, resid.shape[1] // block, one, 0)
        done += resid.shape[1]
    for i, piece in enumerate(outs):
        piece[...] = out[i].astype(piece.dtype)


def final_kernel(plan, pooled, left, right, held, sems):
    rows, n = left.shape[0], pooled.shape[0]
    parts = split3(pooled[...])
    at = lax.broadcasted_iota(jnp.int32, (rows, n), 0)
    copies = []
    for side, out in enumerate((left, right)):
        hit = (plan[pl.ds(2 + side, 1), :][:, :n] == at).astype(BF16)
        held[side] = sum(jnp.dot(hit, part, preferred_element_type=F32) for part in parts)
        copies.append(pltpu.make_async_copy(held.at[side], out, sems.at[side]))
        copies[-1].start()
    for copy in copies:
        copy.wait()


ANY = pl.BlockSpec(memory_space=pl.ANY)
IN_VMEM = pl.BlockSpec(memory_space=pltpu.VMEM)
IN_SMEM = pl.BlockSpec(memory_space=pltpu.SMEM)
LIMIT = pltpu.CompilerParams(vmem_limit_bytes=6 * 1024 * 1024)
WIDE_LIMIT = pltpu.CompilerParams(vmem_limit_bytes=24 * 1024 * 1024)


def shape(dims, kind):
    return jax.ShapeDtypeStruct(dims, kind)


def held_in_vmem(array):
    return pltpu.with_memory_space_constraint(array, pltpu.VMEM)


def qkv(xs, first, gain, weights, loads, keep, before, resid, pair_rows, extra=None, after=(), cost=COST):
    rows, wide = sum(x.shape[0] for x in xs), xs[0].shape[1]
    total = sum(w.shape[1] for w in weights)
    args = [*xs, gain, *weights] + (before or [])
    in_specs = [IN_VMEM] * (len(xs) + 1) + [ANY if loads else IN_VMEM] * 3
    in_specs += [IN_VMEM] * len(before or [])
    out_shape = [shape((rows, total), F32), shape((rows, LANES), F32)]
    scratch = []
    if resid:
        out_shape.append(shape((xs[0].shape[0] // pair_rows, wide), F32))
    if loads:
        halves = [pltpu.VMEM((wide, w.shape[1]), w.dtype) for w in weights]
        if keep:
            out_shape += halves
        else:
            scratch += halves
        scratch.append(pltpu.SemaphoreType.DMA((3, wide // BLOCK)))
    if extra is not None:
        array, part, at = extra
        args.append(array)
        in_specs.append(ANY)
        out_shape.append(pltpu.VMEM((part, array.shape[1]), array.dtype))
        scratch.append(pltpu.SemaphoreType.DMA(()))
    args += after
    in_specs += [ANY] * len(after)
    out = pl.pallas_call(
        functools.partial(
            qkv_kernel,
            len(xs),
            first,
            loads,
            keep,
            None if extra is None else extra[2],
            before is not None,
            resid,
            len(after),
            pair_rows,
        ),
        in_specs=in_specs,
        out_specs=[IN_VMEM] * len(out_shape),
        out_shape=out_shape,
        scratch_shapes=scratch,
        compiler_params=LIMIT if keep or not loads else WIDE_LIMIT,
        cost_estimate=pl.CostEstimate(
            flops=cost * wide * total, bytes_accessed=2 * rows * wide, transcendentals=0
        ),
    )(*args)
    out = list(out)
    result = {"sums": [out.pop(0), out.pop(0)]}
    if resid:
        result["resid"] = out.pop(0)
    if keep:
        result["weights"] = [held_in_vmem(out.pop(0)) for _ in range(3)]
    if extra is not None:
        result["extra"] = held_in_vmem(out.pop(0))
    return result


def on_device(
    left_table,
    right_table,
    left_owner,
    left_row,
    right_owner,
    right_row,
    pair_count,
    norm_gain,
    query_weight,
    key_weight,
    value_weight,
    output_weight,
):
    groups = lax.axis_size("group")
    tensors = lax.axis_size("tensor")
    group, tensor = lax.axis_index("group"), lax.axis_index("tensor")
    pairs_here = left_owner.shape[0]
    rows_here, toks, width = left_table.shape
    share, cap = plan_sizes(groups, pairs_here)
    cells, items = groups * cap, 2 * share
    rows = items * toks
    pair_rows = 2 * toks
    length = pair_rows * tensors
    features = width // tensors
    n = groups * pairs_here

    code = (left_owner[:, 0] * rows_here + left_row) | (
        (right_owner[:, 0] * rows_here + right_row) << RIGHT_SHIFT
    )
    code = jnp.where(jnp.arange(pairs_here, dtype=jnp.int32) < pair_count[0], code, DEAD)
    at = jnp.arange(n, dtype=jnp.int32) // pairs_here
    code = jnp.where(at == group, jnp.tile(code, groups), 0)[None, :]
    hop = 1
    while hop < groups:
        codes = [code, lax.ppermute(code, "group", [(i, i ^ hop) for i in range(groups)])]
        code, hop = codes[0] + codes[1], 2 * hop

    head = width * 5 // 8
    parts = ((0, head), (head, width - head))
    me = jnp.reshape(group, (1,)).astype(jnp.int32)
    plan, cell_rows = pl.pallas_call(
        functools.partial(plan_kernel, groups, share, cap, rows_here, parts[0][1]),
        in_specs=[IN_SMEM, IN_VMEM, IN_VMEM, ANY, ANY],
        out_specs=[IN_VMEM, IN_VMEM],
        out_shape=[shape((8, LANES), jnp.int32), shape((cells, toks, parts[0][1]), BF16)],
        scratch_shapes=[
            pltpu.SMEM((8, LANES), jnp.int32),
            pltpu.SemaphoreType.DMA(()),
            pltpu.SemaphoreType.DMA((cells,)),
        ],
        compiler_params=LIMIT,
    )(me, *codes, left_table, right_table)
    sends = [cell_rows]
    for first, wide in parts[1:]:
        sends.append(
            pl.pallas_call(
                functools.partial(gather_kernel, rows_here, cells, first, wide),
                in_specs=[IN_SMEM, ANY, ANY],
                out_specs=IN_VMEM,
                out_shape=shape((cells, toks, wide), BF16),
                scratch_shapes=[pltpu.SemaphoreType.DMA((cells,))],
                compiler_params=LIMIT,
            )(plan, left_table, right_table)
        )
    gain = norm_gain[None, :]
    weights = [
        pltpu.with_memory_space_constraint(w, pltpu.HBM)
        for w in (query_weight, key_weight, value_weight)
    ]
    ring = [(i, (i + 1) % tensors) for i in range(tensors)]

    def exchange(send):
        return lax.all_to_all(send, "group", split_axis=0, concat_axis=0, tiled=True)

    def pick(got, after):
        wide = got.shape[2]
        return pl.pallas_call(
            functools.partial(pick_kernel, items, len(after)),
            in_specs=[IN_SMEM, ANY] + [ANY] * len(after),
            out_specs=IN_VMEM,
            out_shape=shape((rows, wide), BF16),
            scratch_shapes=[
                pltpu.VMEM((items, toks, wide), BF16),
                pltpu.SemaphoreType.DMA((items,)),
            ],
            compiler_params=LIMIT,
        )(plan, got, *after)

    def pass_on(x):
        return lax.ppermute(x, "tensor", ring)

    def both(x, other):
        return lax.optimization_barrier((x, other))[0]

    def part_one(low, high, kept, extra=None, after=(), cost=COST):
        return qkv(
            one[low:high],
            parts[0][0],
            gain,
            kept or weights,
            not kept,
            low == 1,
            None,
            low == 0,
            pair_rows,
            extra,
            after,
            cost,
        )

    def part_two(low, high, kept, before, extra=None, after=(), cost=COST):
        return qkv(
            two[low:high],
            parts[1][0],
            gain,
            kept or weights,
            not kept,
            not kept,
            before["sums"],
            low == 0,
            pair_rows,
            extra,
            after,
            cost,
        )

    one = [pick(exchange(sends[0]), [])]
    first = part_one(0, 1, None)
    one.append(pass_on(one[0]))
    two = [pick(exchange(sends[1]), [first["sums"][1], one[1]])]
    for _ in range(2, tensors):
        one.append(pass_on(one[-1]))
    deep = output_weight.shape[0] // WO_PARTS
    next_one = part_one(1, 3, None, None, [two[0]])
    two.append(both(pass_on(two[0]), next_one["sums"][1]))
    first_two = part_two(0, 1, None, first, None, [two[1]])
    for _ in range(2, tensors):
        two.append(pass_on(two[-1]))
    next_two = part_two(1, 3, first_two["weights"], next_one, None, (), 0)
    rest = []
    for at in range(3, tensors):
        rest.append(
            part_one(
                at,
                at + 1,
                next_one["weights"],
                (output_weight, deep, 0) if at == 3 else None,
                [next_two["sums"][1]],
            )
        )
        if at + 1 < tensors:
            rest[-1]["sums"] = part_two(at, at + 1, first_two["weights"], rest[-1])["sums"]
    sums = [x["sums"] for x in [first_two, next_two] + rest]
    shards, resids = sums, [first["resid"], first_two["resid"]]
    wos = [rest[0]["extra"], output_weight]
    held, held_weights = two, [first_two["weights"]]
    accs, sqs = [s[0] for s in sums], [s[1] for s in sums]

    args = [held[-1], gain, *held_weights[-1], *wos, *accs, *sqs, *resids]
    in_specs = [IN_SMEM] + [IN_VMEM] * len(args)
    in_specs[7] = ANY
    partial_sums = pl.pallas_call(
        functools.partial(
            tail_kernel, tensors, len(shards), len(parts), width, length, pair_rows, parts[-1][0]
        ),
        in_specs=in_specs,
        out_specs=[IN_VMEM] * tensors,
        out_shape=[shape((share, features), F32)]
        + [shape((share, features), BF16)] * (tensors - 1),
        scratch_shapes=[
            pltpu.VMEM((2 * share, output_weight.shape[0]), BF16),
            pltpu.VMEM((tensors, share, features), F32),
            pltpu.VMEM((deep, width), BF16),
            pltpu.SemaphoreType.DMA((LOADS,)),
        ],
        compiler_params=WIDE_LIMIT,
        cost_estimate=pl.CostEstimate(
            flops=32 * share * width * output_weight.shape[0],
            bytes_accessed=2 * rows * width,
            transcendentals=0,
        ),
    )(jnp.reshape(tensor, (1,)).astype(jnp.int32), *args)
    pooled = partial_sums[0]
    for step in range(1, tensors):
        swap = [(i, i ^ step) for i in range(tensors)]
        pooled = pooled + lax.ppermute(partial_sums[step], "tensor", swap).astype(F32)
    everyone = lax.all_gather(pooled, "group", tiled=True)

    def fast():
        return tuple(
            pl.pallas_call(
                final_kernel,
                in_specs=[IN_VMEM, IN_VMEM],
                out_specs=[ANY, ANY],
                out_shape=[pltpu.HBM((rows_here, features), F32)] * 2,
                scratch_shapes=[
                    pltpu.VMEM((2, rows_here, features), F32),
                    pltpu.SemaphoreType.DMA((2,)),
                ],
                compiler_params=LIMIT,
            )(plan, everyone)
        )

    def general():
        return general_program(
            left_table,
            right_table,
            left_owner,
            left_row,
            right_owner,
            right_row,
            pair_count,
            norm_gain,
            query_weight,
            key_weight,
            value_weight,
            output_weight,
        )

    return lax.cond(plan[4, 0] > 0, general, fast)


def solution(mesh):
    return jax.shard_map(
        on_device,
        mesh=mesh,
        in_specs=(
            P("group", "tensor", None),
            P("group", "tensor", None),
            P("group", None),
            P("group"),
            P("group", None),
            P("group"),
            P("group"),
            P(),
            P(None, "tensor"),
            P(None, "tensor"),
            P(None, "tensor"),
            P("tensor", None),
        ),
        out_specs=(P("group", "tensor"), P("group", "tensor")),
        check_vma=False,
    )
```

```python
import functools

import jax
import jax.numpy as jnp
from jax import lax
from jax.experimental import pallas as pl
from jax.experimental.pallas import tpu as pltpu
from jax.sharding import PartitionSpec as P

HEAD_DIM = 128


score_scale = 4.0


def slot_plan(owner, groups, capacity):
    count = owner.shape[0]
    order = jnp.arange(count, dtype=jnp.int32)
    same_owner = owner[:, None] == owner[None, :]
    earlier = order[None, :] < order[:, None]
    rank = jnp.sum(jnp.logical_and(same_owner, earlier), axis=1)
    owner_hit = owner[:, None, None] == jnp.arange(groups, dtype=jnp.int32)[None, :, None]
    rank_hit = rank[:, None, None] == jnp.arange(capacity, dtype=jnp.int32)[None, None, :]
    return (rank, jnp.logical_and(owner_hit, rank_hit))


def request_ids(slot_match, row_index):
    return jnp.sum(jnp.where(slot_match, row_index[:, None, None], 0), axis=0)


def owner_sums(row_ids, arrived, rows_here):
    onehot = (row_ids[:, :, None] == jnp.arange(rows_here, dtype=jnp.int32)[None, None, :]).astype(
        jnp.float32
    )
    return jnp.einsum("gcr,gcf->rf", onehot, arrived, precision=lax.Precision.HIGHEST)


def general_program(
    left_table,
    right_table,
    left_owner,
    left_row,
    right_owner,
    right_row,
    pair_count,
    norm_gain,
    query_weight,
    key_weight,
    value_weight,
    output_weight,
):
    groups = lax.axis_size("group")
    tensors = lax.axis_size("tensor")
    pairs_here = left_owner.shape[0]
    capacity = 2 * pairs_here // groups
    rows_here = left_table.shape[0]
    width = left_table.shape[2]
    feature_share = width // tensors
    left_group = left_owner[:, 0]
    right_group = right_owner[:, 0]
    left_rank, left_match = slot_plan(left_group, groups, capacity)
    right_rank, right_match = slot_plan(right_group, groups, capacity)
    left_request = request_ids(left_match, left_row)
    right_request = request_ids(right_match, right_row)
    left_spread = jnp.broadcast_to(left_request[:, None, :], (groups, tensors, capacity)).reshape(
        groups * tensors, capacity
    )
    right_spread = jnp.broadcast_to(right_request[:, None, :], (groups, tensors, capacity)).reshape(
        groups * tensors, capacity
    )
    left_wanted, right_wanted = (
        lax.all_to_all(left_spread, ("group", "tensor"), split_axis=0, concat_axis=0, tiled=True),
        lax.all_to_all(right_spread, ("group", "tensor"), split_axis=0, concat_axis=0, tiled=True),
    )
    left_back, right_back = (
        lax.all_to_all(
            left_table[left_wanted], ("group", "tensor"), split_axis=0, concat_axis=0, tiled=True
        ),
        lax.all_to_all(
            right_table[right_wanted], ("group", "tensor"), split_axis=0, concat_axis=0, tiled=True
        ),
    )
    left_back = left_back.reshape(groups, tensors, capacity, left_table.shape[1], width)
    right_back = right_back.reshape(groups, tensors, capacity, right_table.shape[1], width)
    left_tokens = left_back[left_group, :, left_rank].reshape(
        pairs_here, tensors * left_table.shape[1], width
    )
    right_tokens = right_back[right_group, :, right_rank].reshape(
        pairs_here, tensors * right_table.shape[1], width
    )
    left_owned = left_wanted.reshape(groups, tensors, capacity)[:, 0]
    right_owned = right_wanted.reshape(groups, tensors, capacity)[:, 0]
    inputs = jnp.concatenate([left_tokens, right_tokens], axis=1)
    length = inputs.shape[1]
    flat = inputs.reshape(pairs_here * length, width)
    wide = flat.astype(jnp.float32)
    scale = lax.rsqrt(jnp.mean(wide * wide, axis=-1, keepdims=True) + 1e-05)
    normed = (wide * scale * norm_gain[None, :]).astype(jnp.bfloat16)
    q_raw = jnp.dot(normed, query_weight, preferred_element_type=jnp.float32)
    k_raw = jnp.dot(normed, key_weight, preferred_element_type=jnp.float32)
    values = jnp.dot(normed, value_weight, preferred_element_type=jnp.float32).astype(jnp.bfloat16)
    kv_local = key_weight.shape[1] // HEAD_DIM
    share = query_weight.shape[1] // HEAD_DIM // kv_local
    q_heads = q_raw.reshape(pairs_here * length, kv_local * share, HEAD_DIM)
    k_heads = k_raw.reshape(pairs_here * length, kv_local, HEAD_DIM)
    q_norm = (
        q_heads * lax.rsqrt(jnp.mean(q_heads * q_heads, axis=-1, keepdims=True) + 1e-06)
    ).astype(jnp.bfloat16)
    k_norm = (
        k_heads * lax.rsqrt(jnp.mean(k_heads * k_heads, axis=-1, keepdims=True) + 1e-06)
    ).astype(jnp.bfloat16)
    q_five = q_norm.reshape(pairs_here, length, kv_local, share, HEAD_DIM)
    k_four = k_norm.reshape(pairs_here, length, kv_local, HEAD_DIM)
    v_four = values.reshape(pairs_here, length, kv_local, HEAD_DIM)
    scores = jnp.einsum("pqkgd,pskd->pkgqs", q_five, k_four, preferred_element_type=jnp.float32) * (
        score_scale / HEAD_DIM
    )
    expo = jnp.exp(scores)
    weights = (expo / jnp.sum(expo, axis=-1, keepdims=True)).astype(jnp.bfloat16)
    context = jnp.einsum(
        "pkgqs,pskd->pqkgd", weights, v_four, preferred_element_type=jnp.float32
    ).astype(jnp.bfloat16)
    context = context.reshape(pairs_here * length, kv_local * share * HEAD_DIM)
    attended = jnp.dot(context, output_weight, preferred_element_type=jnp.float32)
    head_term = jnp.mean(attended.reshape(pairs_here, length, width), axis=1)
    shares = head_term.reshape(pairs_here, tensors, feature_share).swapaxes(0, 1)
    shares = lax.all_to_all(shares, "tensor", split_axis=0, concat_axis=0, tiled=True)
    head_part = jnp.sum(shares, axis=0)
    feature_start = lax.axis_index("tensor") * feature_share
    own_features = lax.dynamic_slice_in_dim(inputs, feature_start, feature_share, 2)
    residual_mean = jnp.mean(own_features.astype(jnp.float32), axis=1)
    live = jnp.arange(pairs_here, dtype=jnp.int32) < pair_count[0]
    pooled = jnp.where(live[:, None], residual_mean + head_part, jnp.zeros_like(head_part))
    left_send = jnp.einsum(
        "pgc,pf->gcf", left_match.astype(jnp.float32), pooled, precision=lax.Precision.HIGHEST
    )
    right_send = jnp.einsum(
        "pgc,pf->gcf", right_match.astype(jnp.float32), pooled, precision=lax.Precision.HIGHEST
    )
    left_got, right_got = (
        lax.all_to_all(left_send, "group", split_axis=0, concat_axis=0, tiled=True),
        lax.all_to_all(right_send, "group", split_axis=0, concat_axis=0, tiled=True),
    )
    left_sums = owner_sums(left_owned, left_got, rows_here)
    right_sums = owner_sums(right_owned, right_got, rows_here)
    return (left_sums, right_sums)

LANES = 128
DEAD = -1
RIGHT_SHIFT = 12
DEALS = (43, 21, 34, 1, 15, 10, 61, 5, 7, 50, 11, 4)
LOADS = 8
BLOCK = 512
COST = 512
WO_PARTS = 2
BF16 = jnp.bfloat16
F32 = jnp.float32


def log2(number):
    bits = number.bit_length() - 1
    assert 1 << bits == number
    return bits


def plan_sizes(groups, pairs_here):
    share = pairs_here // 2
    mean = -(-2 * share // groups)
    return (share, min(LANES // groups, (5 * mean + 1) // 2))


def column(row):
    n = row.shape[1]
    return jnp.transpose(jnp.broadcast_to(row, (n, n)))[:, :1]


def split3(wide):
    high = wide.astype(BF16)
    rest = wide - high.astype(F32)
    mid = rest.astype(BF16)
    low = (rest - mid.astype(F32)).astype(BF16)
    return (high, mid, low)


def plan_body(codes, me, groups, share, cap, rows_here):
    n = codes.shape[1]
    gbits, rbits = log2(groups), log2(rows_here)
    live_total = groups * share
    live = codes >= 0
    left = jnp.where(live, codes & ((1 << RIGHT_SHIFT) - 1), 0)
    right = jnp.where(live, codes >> RIGHT_SHIFT, 0)
    left_own, right_own = left >> rbits, right >> rbits
    order = lax.broadcasted_iota(jnp.int32, (1, n), 1)
    owners = lax.broadcasted_iota(jnp.int32, (groups, n), 0)
    load_of = (left_own == owners).astype(F32) + (right_own == owners).astype(F32)
    load_of = jnp.where(live, load_of, 0.0).astype(BF16)
    live_c, left_c, right_c = column(live.astype(jnp.int32)), column(left), column(right)
    lo_c, ro_c = left_c >> rbits, right_c >> rbits
    order_c = lax.broadcasted_iota(jnp.int32, (n, 1), 0)

    def key(one, other, alive, at, deal):
        major, minor = (other, one) if deal >> 5 else (one, other)
        minor = (minor * (2 * ((deal >> 3) & 3) + 1) + (deal & 7) * major) & (groups - 1)
        return jnp.where(alive, ((major << gbits) + minor) * n, groups * groups * n) + at

    best, best_load = None, None
    for deal in DEALS:
        key_r = key(left_own, right_own, live, order, deal)
        key_c = key(lo_c, ro_c, live_c > 0, order_c, deal)
        rank = jnp.sum((key_c < key_r).astype(jnp.int32), axis=0, keepdims=True)
        to = jnp.where(rank < live_total, rank & (groups - 1), groups)
        hit = (to == owners).astype(BF16)
        load = lax.dot_general(hit, load_of, (((1,), (1,)), ((), ())), preferred_element_type=F32)
        most = jnp.max(jnp.max(load, axis=1, keepdims=True), axis=0, keepdims=True)
        if best is None:
            best, best_load = rank, most
        else:
            better = most < best_load
            best = jnp.where(better, rank, best)
            best_load = jnp.where(better, most, best_load)
    rank = best
    rank_c = column(rank)
    to_c = jnp.where(rank_c < live_total, rank_c & (groups - 1), groups)
    slot_c = rank_c >> gbits
    to = jnp.where(rank < live_total, rank & (groups - 1), groups)
    same_to = to_c == to
    earlier = jnp.logical_and(same_to, rank < rank_c)

    def count(mask):
        return jnp.sum(mask.astype(jnp.int32), axis=1, keepdims=True)

    left_pos = count(jnp.logical_and(earlier, lo_c == left_own))
    right_pos = count(jnp.logical_and(earlier, ro_c == right_own)) + count(
        jnp.logical_and(jnp.logical_and(same_to, rank < live_total), ro_c == left_own)
    )
    lane = lax.broadcasted_iota(jnp.int32, (n, LANES), 1)
    alive = rank_c < live_total

    def place(mask, at, value):
        return jnp.sum(
            jnp.where(jnp.logical_and(mask, at == lane), value, 0), axis=0, keepdims=True
        )

    left_in = jnp.logical_and(alive, left_pos < cap)
    right_in = jnp.logical_and(alive, right_pos < cap)
    local_left, local_right = left_c & (rows_here - 1), right_c & (rows_here - 1)
    send = place(
        jnp.logical_and(left_in, lo_c == me), to_c * cap + left_pos, local_left + 1
    ) + place(
        jnp.logical_and(right_in, ro_c == me), to_c * cap + right_pos, local_right + rows_here + 1
    )
    mine = jnp.logical_and(alive, to_c == me)
    fetch = place(
        jnp.logical_and(mine, left_in), slot_c * 2, lo_c * cap + left_pos
    ) + place(jnp.logical_and(mine, right_in), slot_c * 2 + 1, ro_c * cap + right_pos)
    back = to_c * share + slot_c
    left_row = place(jnp.logical_and(alive, lo_c == me), back, local_left + 1) - 1
    right_row = place(jnp.logical_and(alive, ro_c == me), back, local_right + 1) - 1
    over = jnp.broadcast_to((best_load > cap).astype(jnp.int32), (1, LANES))
    return (send, fetch, left_row, right_row, over)


def gather_cells(plan, left, right, out, sems, rows_here, cells, first, wide):
    def begin(cell, carry):
        index = plan[0, cell] - 1
        row = index & (rows_here - 1)
        for side, table in ((0, left), (1, right)):

            @pl.when(jnp.logical_and(index >= side * rows_here, index < (side + 1) * rows_here))
            def _():
                pltpu.make_async_copy(
                    table.at[row, :, pl.ds(first, wide)], out.at[cell], sems.at[cell]
                ).start()

        return carry

    def finish(cell, carry):
        @pl.when(plan[0, cell] > 0)
        def _():
            pltpu.make_async_copy(
                left.at[0, :, pl.ds(first, wide)], out.at[cell], sems.at[cell]
            ).wait()

        return carry

    lax.fori_loop(0, cells, begin, 0)
    lax.fori_loop(0, cells, finish, 0)


def plan_kernel(groups, share, cap, rows_here, wide, me, mine, others, left, right, plan_out, out, plan, sem, sems):
    rows = mine[...] + others[...]
    table = plan_body(rows, me[0], groups, share, cap, rows_here)
    for at, row in enumerate(table):
        plan_out[pl.ds(at, 1), :] = row
    copy = pltpu.make_async_copy(plan_out, plan, sem)
    copy.start()
    copy.wait()
    gather_cells(plan, left, right, out, sems, rows_here, groups * cap, 0, wide)


def gather_kernel(rows_here, cells, first, wide, plan, left, right, out, sems):
    gather_cells(plan, left, right, out, sems, rows_here, cells, first, wide)


def pick_kernel(items, after, plan, got, *refs):
    out, held, sems = refs[after:]

    def begin(item, carry):
        pltpu.make_async_copy(got.at[plan[1, item]], held.at[item], sems.at[item]).start()
        return carry

    def finish(item, carry):
        pltpu.make_async_copy(got.at[0], held.at[item], sems.at[item]).wait()
        return carry

    lax.fori_loop(0, items, begin, 0)
    lax.fori_loop(0, items, finish, 0)
    out[...] = held[...].reshape(out.shape)


def products(x_refs, gain, weights, first, ready=None):
    rows, wide = sum(x.shape[0] for x in x_refs), x_refs[0].shape[1]
    block = BLOCK if ready is not None else 2 * BLOCK
    widths = [w.shape[1] for w in weights]

    def one(i, carry):
        sums, square = carry
        if ready is not None:
            ready(i)
        at = pl.multiple_of(i * block, block)
        x = jnp.concatenate([x[:, pl.ds(at, block)] for x in x_refs], axis=0).astype(F32)
        normed = (x * gain[:, pl.ds(first + at, block)]).astype(BF16)
        sums = tuple(
            total + jnp.dot(normed, w[pl.ds(at, block), :], preferred_element_type=F32)
            for total, w in zip(sums, weights)
        )
        return (sums, square + jnp.sum(x * x, axis=1, keepdims=True))

    zero = (tuple(jnp.zeros((rows, n), F32) for n in widths), jnp.zeros((rows, 1), F32))
    sums, square = lax.fori_loop(0, wide // block, one, zero)
    return (jnp.concatenate(sums, axis=1), square)


def qkv_kernel(shards, first, loads, keep, extra, more, resid, after, pair_rows, *refs):
    refs = list(refs)
    x_refs = [refs.pop(0) for _ in range(shards)]
    gain = refs.pop(0)
    sources = [refs.pop(0) for _ in range(3)]
    before = [refs.pop(0) for _ in range(2)] if more else None
    extra_source = refs.pop(0) if extra is not None else None
    del refs[:after]
    sums_out, square_out = refs.pop(0), refs.pop(0)
    resid_out = refs.pop(0) if resid else None
    ready, weights = None, sources
    if keep:
        weights = [refs.pop(0) for _ in range(3)]
    extra_held = refs.pop(0) if extra is not None else None
    if loads and not keep:
        weights = [refs.pop(0) for _ in range(3)]
    if loads:
        sems = refs.pop(0)
        block = BLOCK

        def copy(which, i):
            at = i * block
            return pltpu.make_async_copy(
                sources[which].at[pl.ds(first + at, block)],
                weights[which].at[pl.ds(at, block)],
                sems.at[which, i],
            )

        for i in range(x_refs[0].shape[1] // block):
            for which in range(3):
                copy(which, i).start()

        def ready(i):
            for which in range(3):
                copy(which, i).wait()

    if extra is not None:
        extra_copy = pltpu.make_async_copy(
            extra_source.at[pl.ds(extra, extra_held.shape[0])], extra_held, refs.pop(0)
        )
        extra_copy.start()
    sums, square = products(x_refs, gain, weights, first, ready)
    square = jnp.broadcast_to(square, (square.shape[0], LANES))
    if more:
        sums += before[0][...]
        square += before[1][...]
    sums_out[...] = sums
    square_out[...] = square
    if resid:
        rows = x_refs[0].shape[0]
        pairs = rows // pair_rows
        pair = lax.broadcasted_iota(jnp.int32, (pairs, rows), 1) // pair_rows
        mine = (pair == lax.broadcasted_iota(jnp.int32, (pairs, rows), 0)).astype(BF16)
        resid_out[...] = jnp.dot(mine, x_refs[0][...], preferred_element_type=F32)
    if extra is not None:
        extra_copy.wait()


def tail_kernel(
    shards, groups, parts, width, length, pair_rows, first, t_ref, x_ref, gain, wq, wk, wv, *refs
):
    wos, refs = refs[:WO_PARTS], refs[WO_PARTS:]
    accs, sqs, resids = refs[:groups], refs[groups : 2 * groups], refs[2 * groups : 2 * groups + parts]
    outs, (ctx, out, wo_tail, sems) = refs[2 * groups + parts : -4], refs[-4:]
    deep = wo_tail.shape[0]
    copies = [
        pltpu.make_async_copy(
            wos[1].at[pl.ds(deep + i * (deep // LOADS), deep // LOADS)],
            wo_tail.at[pl.ds(i * (deep // LOADS), deep // LOADS)],
            sems.at[i],
        )
        for i in range(LOADS)
    ]
    for copy in copies:
        copy.start()
    wos = [wos[0], wo_tail]
    pairs, features = out.shape[1:]
    heads, kv_heads = wq.shape[1] // HEAD_DIM, wk.shape[1] // HEAD_DIM
    share = heads // kv_heads
    sums, square = products([x_ref], gain, (wq, wk, wv), first)
    acc = jnp.concatenate([a[...] for a in accs[:-1]] + [accs[-1][...] + sums], axis=0)
    sq = jnp.concatenate([s[:, :1] for s in sqs[:-1]] + [sqs[-1][:, :1] + square], axis=0)
    tokens = acc.shape[0]
    acc = acc * lax.rsqrt(sq * (1.0 / width) + 1e-05)
    rows = tokens // shards
    row = lax.broadcasted_iota(jnp.int32, (share * tokens, tokens), 0)
    col = lax.broadcasted_iota(jnp.int32, (share * tokens, tokens), 1)
    same = ((row & (rows - 1)) >> log2(pair_rows)) == ((col & (rows - 1)) >> log2(pair_rows))
    pair = lax.broadcasted_iota(jnp.int32, (pairs, tokens), 0)
    token = lax.broadcasted_iota(jnp.int32, (pairs, tokens), 1)
    member = ((token & (rows - 1)) >> log2(pair_rows)) == pair
    nq, nk = heads * HEAD_DIM, kv_heads * HEAD_DIM

    def unit(part):
        return (part * lax.rsqrt(jnp.mean(part * part, axis=1, keepdims=True) + 1e-06)).astype(
            BF16
        )

    def head(start):
        return acc[:, start : start + HEAD_DIM]

    for kv in range(kv_heads):
        k = unit(head(nq + kv * HEAD_DIM))
        v = head(nq + nk + kv * HEAD_DIM).astype(BF16)
        q = jnp.concatenate(
            [unit(head((kv * share + i) * HEAD_DIM)) for i in range(share)], axis=0
        )
        scores = lax.dot_general(
            q, k, (((1,), (1,)), ((), ())), preferred_element_type=F32
        ) * (score_scale / HEAD_DIM)
        expo = jnp.where(same, jnp.exp(scores), 0.0)
        weights = expo / jnp.sum(expo, axis=1, keepdims=True)
        spread = []
        for i in range(share):
            mean = jnp.sum(weights[i * tokens : (i + 1) * tokens], axis=0, keepdims=True)
            spread.append(jnp.where(member, mean * (1.0 / length), 0.0))
        spread = jnp.concatenate(spread, axis=0)
        high = spread.astype(BF16)
        low = (spread - high.astype(F32)).astype(BF16)
        context = jnp.dot(
            jnp.concatenate([high, low], axis=0), v, preferred_element_type=F32
        )
        context = context[: share * pairs] + context[share * pairs :]
        for i in range(share):
            one_head = context[i * pairs : (i + 1) * pairs]
            high = one_head.astype(BF16)
            low = (one_head - high.astype(F32)).astype(BF16)
            at = (kv * share + i) * HEAD_DIM
            ctx[:, at : at + HEAD_DIM] = jnp.concatenate([high, low], axis=0)

    for copy in copies:
        copy.wait()
    block = min(2 * BLOCK, features)
    per = features // block
    done = 0
    for resid in resids:

        def one(i, carry):
            here = pl.multiple_of(i * block, block)
            i = i + done // block
            at = pl.multiple_of(i * block, block)
            both = sum(
                jnp.dot(
                    ctx[:, j * deep : (j + 1) * deep],
                    wo[:, pl.ds(at, block)],
                    preferred_element_type=F32,
                )
                for j, wo in enumerate(wos)
            )
            both = both[:pairs] + both[pairs:] + resid[:, pl.ds(here, block)] * (1.0 / length)
            inside = pl.multiple_of((i % per) * block, block)
            out[pl.ds((i // per) ^ t_ref[0], 1), :, pl.ds(inside, block)] = both[None]
            return carry

        lax.fori_loop(0, resid.shape[1] // block, one, 0)
        done += resid.shape[1]
    for i, piece in enumerate(outs):
        piece[...] = out[i].astype(piece.dtype)


def final_kernel(plan, pooled, left, right, held, sems):
    rows, n = left.shape[0], pooled.shape[0]
    parts = split3(pooled[...])
    at = lax.broadcasted_iota(jnp.int32, (rows, n), 0)
    copies = []
    for side, out in enumerate((left, right)):
        hit = (plan[pl.ds(2 + side, 1), :][:, :n] == at).astype(BF16)
        held[side] = sum(jnp.dot(hit, part, preferred_element_type=F32) for part in parts)
        copies.append(pltpu.make_async_copy(held.at[side], out, sems.at[side]))
        copies[-1].start()
    for copy in copies:
        copy.wait()


ANY = pl.BlockSpec(memory_space=pl.ANY)
IN_VMEM = pl.BlockSpec(memory_space=pltpu.VMEM)
IN_SMEM = pl.BlockSpec(memory_space=pltpu.SMEM)
LIMIT = pltpu.CompilerParams(vmem_limit_bytes=6 * 1024 * 1024)
WIDE_LIMIT = pltpu.CompilerParams(vmem_limit_bytes=24 * 1024 * 1024)


def shape(dims, kind):
    return jax.ShapeDtypeStruct(dims, kind)


def held_in_vmem(array):
    return pltpu.with_memory_space_constraint(array, pltpu.VMEM)


def qkv(xs, first, gain, weights, loads, keep, before, resid, pair_rows, extra=None, after=(), cost=COST):
    rows, wide = sum(x.shape[0] for x in xs), xs[0].shape[1]
    total = sum(w.shape[1] for w in weights)
    args = [*xs, gain, *weights] + (before or [])
    in_specs = [IN_VMEM] * (len(xs) + 1) + [ANY if loads else IN_VMEM] * 3
    in_specs += [IN_VMEM] * len(before or [])
    out_shape = [shape((rows, total), F32), shape((rows, LANES), F32)]
    scratch = []
    if resid:
        out_shape.append(shape((xs[0].shape[0] // pair_rows, wide), F32))
    if loads:
        halves = [pltpu.VMEM((wide, w.shape[1]), w.dtype) for w in weights]
        if keep:
            out_shape += halves
        else:
            scratch += halves
        scratch.append(pltpu.SemaphoreType.DMA((3, wide // BLOCK)))
    if extra is not None:
        array, part, at = extra
        args.append(array)
        in_specs.append(ANY)
        out_shape.append(pltpu.VMEM((part, array.shape[1]), array.dtype))
        scratch.append(pltpu.SemaphoreType.DMA(()))
    args += after
    in_specs += [ANY] * len(after)
    out = pl.pallas_call(
        functools.partial(
            qkv_kernel,
            len(xs),
            first,
            loads,
            keep,
            None if extra is None else extra[2],
            before is not None,
            resid,
            len(after),
            pair_rows,
        ),
        in_specs=in_specs,
        out_specs=[IN_VMEM] * len(out_shape),
        out_shape=out_shape,
        scratch_shapes=scratch,
        compiler_params=LIMIT if keep or not loads else WIDE_LIMIT,
        cost_estimate=pl.CostEstimate(
            flops=cost * wide * total, bytes_accessed=2 * rows * wide, transcendentals=0
        ),
    )(*args)
    out = list(out)
    result = {"sums": [out.pop(0), out.pop(0)]}
    if resid:
        result["resid"] = out.pop(0)
    if keep:
        result["weights"] = [held_in_vmem(out.pop(0)) for _ in range(3)]
    if extra is not None:
        result["extra"] = held_in_vmem(out.pop(0))
    return result


def on_device(
    left_table,
    right_table,
    left_owner,
    left_row,
    right_owner,
    right_row,
    pair_count,
    norm_gain,
    query_weight,
    key_weight,
    value_weight,
    output_weight,
):
    groups = lax.axis_size("group")
    tensors = lax.axis_size("tensor")
    group, tensor = lax.axis_index("group"), lax.axis_index("tensor")
    pairs_here = left_owner.shape[0]
    rows_here, toks, width = left_table.shape
    share, cap = plan_sizes(groups, pairs_here)
    cells, items = groups * cap, 2 * share
    rows = items * toks
    pair_rows = 2 * toks
    length = pair_rows * tensors
    features = width // tensors
    n = groups * pairs_here

    code = (left_owner[:, 0] * rows_here + left_row) | (
        (right_owner[:, 0] * rows_here + right_row) << RIGHT_SHIFT
    )
    code = jnp.where(jnp.arange(pairs_here, dtype=jnp.int32) < pair_count[0], code, DEAD)
    at = jnp.arange(n, dtype=jnp.int32) // pairs_here
    code = jnp.where(at == group, jnp.tile(code, groups), 0)[None, :]
    hop = 1
    while hop < groups:
        codes = [code, lax.ppermute(code, "group", [(i, i ^ hop) for i in range(groups)])]
        code, hop = codes[0] + codes[1], 2 * hop

    head = width * 5 // 8
    parts = ((0, head), (head, width - head))
    me = jnp.reshape(group, (1,)).astype(jnp.int32)
    plan, cell_rows = pl.pallas_call(
        functools.partial(plan_kernel, groups, share, cap, rows_here, parts[0][1]),
        in_specs=[IN_SMEM, IN_VMEM, IN_VMEM, ANY, ANY],
        out_specs=[IN_VMEM, IN_VMEM],
        out_shape=[shape((8, LANES), jnp.int32), shape((cells, toks, parts[0][1]), BF16)],
        scratch_shapes=[
            pltpu.SMEM((8, LANES), jnp.int32),
            pltpu.SemaphoreType.DMA(()),
            pltpu.SemaphoreType.DMA((cells,)),
        ],
        compiler_params=LIMIT,
    )(me, *codes, left_table, right_table)
    sends = [cell_rows]
    for first, wide in parts[1:]:
        sends.append(
            pl.pallas_call(
                functools.partial(gather_kernel, rows_here, cells, first, wide),
                in_specs=[IN_SMEM, ANY, ANY],
                out_specs=IN_VMEM,
                out_shape=shape((cells, toks, wide), BF16),
                scratch_shapes=[pltpu.SemaphoreType.DMA((cells,))],
                compiler_params=LIMIT,
            )(plan, left_table, right_table)
        )
    gain = norm_gain[None, :]
    weights = [
        pltpu.with_memory_space_constraint(w, pltpu.HBM)
        for w in (query_weight, key_weight, value_weight)
    ]
    ring = [(i, (i + 1) % tensors) for i in range(tensors)]

    def exchange(send):
        return lax.all_to_all(send, "group", split_axis=0, concat_axis=0, tiled=True)

    def pick(got, after):
        wide = got.shape[2]
        return pl.pallas_call(
            functools.partial(pick_kernel, items, len(after)),
            in_specs=[IN_SMEM, ANY] + [ANY] * len(after),
            out_specs=IN_VMEM,
            out_shape=shape((rows, wide), BF16),
            scratch_shapes=[
                pltpu.VMEM((items, toks, wide), BF16),
                pltpu.SemaphoreType.DMA((items,)),
            ],
            compiler_params=LIMIT,
        )(plan, got, *after)

    def pass_on(x):
        return lax.ppermute(x, "tensor", ring)

    def both(x, other):
        return lax.optimization_barrier((x, other))[0]

    def part_one(low, high, kept, extra=None, after=(), cost=COST):
        return qkv(
            one[low:high],
            parts[0][0],
            gain,
            kept or weights,
            not kept,
            low == 1,
            None,
            low == 0,
            pair_rows,
            extra,
            after,
            cost,
        )

    def part_two(low, high, kept, before, extra=None, after=(), cost=COST):
        return qkv(
            two[low:high],
            parts[1][0],
            gain,
            kept or weights,
            not kept,
            not kept,
            before["sums"],
            low == 0,
            pair_rows,
            extra,
            after,
            cost,
        )

    one = [pick(exchange(sends[0]), [])]
    first = part_one(0, 1, None)
    one.append(pass_on(one[0]))
    two = [pick(exchange(sends[1]), [first["sums"][1], one[1]])]
    for _ in range(2, tensors):
        one.append(pass_on(one[-1]))
    deep = output_weight.shape[0] // WO_PARTS
    next_one = part_one(1, 3, None, None, [two[0]])
    two.append(both(pass_on(two[0]), next_one["sums"][1]))
    first_two = part_two(0, 1, None, first, None, [two[1]])
    for _ in range(2, tensors):
        two.append(pass_on(two[-1]))
    next_two = part_two(1, 3, first_two["weights"], next_one, None, (), 0)
    rest = []
    for at in range(3, tensors):
        rest.append(
            part_one(
                at,
                at + 1,
                next_one["weights"],
                (output_weight, deep, 0) if at == 3 else None,
                [next_two["sums"][1]],
            )
        )
        if at + 1 < tensors:
            rest[-1]["sums"] = part_two(at, at + 1, first_two["weights"], rest[-1])["sums"]
    sums = [x["sums"] for x in [first_two, next_two] + rest]
    shards, resids = sums, [first["resid"], first_two["resid"]]
    wos = [rest[0]["extra"], output_weight]
    held, held_weights = two, [first_two["weights"]]
    accs, sqs = [s[0] for s in sums], [s[1] for s in sums]

    args = [held[-1], gain, *held_weights[-1], *wos, *accs, *sqs, *resids]
    in_specs = [IN_SMEM] + [IN_VMEM] * len(args)
    in_specs[7] = ANY
    partial_sums = pl.pallas_call(
        functools.partial(
            tail_kernel, tensors, len(shards), len(parts), width, length, pair_rows, parts[-1][0]
        ),
        in_specs=in_specs,
        out_specs=[IN_VMEM] * tensors,
        out_shape=[shape((share, features), F32)]
        + [shape((share, features), BF16)] * (tensors - 1),
        scratch_shapes=[
            pltpu.VMEM((2 * share, output_weight.shape[0]), BF16),
            pltpu.VMEM((tensors, share, features), F32),
            pltpu.VMEM((deep, width), BF16),
            pltpu.SemaphoreType.DMA((LOADS,)),
        ],
        compiler_params=WIDE_LIMIT,
        cost_estimate=pl.CostEstimate(
            flops=32 * share * width * output_weight.shape[0],
            bytes_accessed=2 * rows * width,
            transcendentals=0,
        ),
    )(jnp.reshape(tensor, (1,)).astype(jnp.int32), *args)
    pooled = partial_sums[0]
    for step in range(1, tensors):
        swap = [(i, i ^ step) for i in range(tensors)]
        pooled = pooled + lax.ppermute(partial_sums[step], "tensor", swap).astype(F32)
    everyone = lax.all_gather(pooled, "group", tiled=True)

    def fast():
        return tuple(
            pl.pallas_call(
                final_kernel,
                in_specs=[IN_VMEM, IN_VMEM],
                out_specs=[ANY, ANY],
                out_shape=[pltpu.HBM((rows_here, features), F32)] * 2,
                scratch_shapes=[
                    pltpu.VMEM((2, rows_here, features), F32),
                    pltpu.SemaphoreType.DMA((2,)),
                ],
                compiler_params=LIMIT,
            )(plan, everyone)
        )

    def general():
        return general_program(
            left_table,
            right_table,
            left_owner,
            left_row,
            right_owner,
            right_row,
            pair_count,
            norm_gain,
            query_weight,
            key_weight,
            value_weight,
            output_weight,
        )

    return lax.cond(plan[4, 0] > 0, general, fast)


def solution(mesh):
    return jax.shard_map(
        on_device,
        mesh=mesh,
        in_specs=(
            P("group", "tensor", None),
            P("group", "tensor", None),
            P("group", None),
            P("group"),
            P("group", None),
            P("group"),
            P("group"),
            P(),
            P(None, "tensor"),
            P(None, "tensor"),
            P(None, "tensor"),
            P("tensor", None),
        ),
        out_specs=(P("group", "tensor"), P("group", "tensor")),
        check_vma=False,
    )
```
